32 devices in a mesh: orbit: 2 (over x), lon: 4 (over y, core), lat: 4 (over z).
Axes of the slice: x: 2, y: 2, z: 4, core: 2. Of those that a mesh axis runs over, the one named last changes fastest.
Arguments:
- observed: float32 [4096, 64], P(('orbit', 'lon', 'lat')), may hold values from -6 to 6
- ray_start: int32 [4096], P(('orbit', 'lon', 'lat')), may hold values from 0 to 2
- tile_cells: int32 [20480, 16], P(('orbit', 'lon', 'lat')), may hold values from 0 to 4095, as said below
- tile_lengths: float32 [20480, 16], P(('orbit', 'lon', 'lat')), may hold values from 0.05 to 0.2
- channel_kernel: float32 [7, 64], replicated, may hold values from -0.75 to 0.75
- noise_weight: float32 [64], replicated, may hold values from 0.25 to 4
- prior_weight: float32 [7], replicated, may hold values from 0.05 to 0.5
Outputs:
- solution_field: float32 [7, 16, 32, 128], P(None, 'lon', 'lat')
- residual: float32 [7, 16, 32, 128], P(None, 'lon', 'lat')
The draws below stay inside these ranges and needn't reach their ends.
Inputs may be any that keep to these rules, and one draw needn't show every extreme that they name: `tile_cells`: each row is a path through the block: its segments move across the block's longitudes at one latitude, their level falling to a tangent level and rising again, one level a segment.
All inputs are finite; a program needn't handle non-finite values.
Results may differ from the reference program's by a relative error of at most 0.0045.
Values sent between devices are 32-bit elements; how exact they have to be, the bound alone decides.
A program may use at most 64 MiB of HBM per device.

```python
import math
import jax
import jax.numpy as jnp
from jax import lax

S = 7
CH = 64
CLON = 4
CLAT = 8
LEV = 128
RAY_DEV = 128
NT = 3
TILE = 16
ITERS = 4
SPAN = 5
NLON = 16
NLAT = 32
NRAY = 4096
N_ORBIT = 2
N_LON = 4
N_LAT = 4


def draw_tile_cells(key, part):
    row_count = N_ORBIT * N_LON * N_LAT * (2 * NT - 1) * RAY_DEV
    keys = jax.random.split(key, 4)
    lat_pick = jax.random.randint(keys[0], (row_count, 1), 0, CLAT)
    lowest = jax.random.randint(keys[1], (row_count, 1), 0, LEV - TILE + 1)
    turning = jax.random.randint(keys[2], (row_count, 1), 0, TILE)
    flipped = jax.random.randint(keys[3], (row_count, 1), 0, 2)
    steps = jnp.arange(TILE, dtype=jnp.int32)[None, :]
    column = steps * CLON // TILE
    column = jnp.where(flipped == 1, CLON - 1 - column, column)
    level = lowest + jnp.abs(steps - turning)
    return ((column * CLAT + lat_pick) * LEV + level).astype(jnp.int32)


def set_ends(entries, own_key, low, largest):
    extent = entries.shape
    spot = [jax.random.randint(jax.random.fold_in(own_key, axis), (), 0, extent[axis]) for axis in range(len(extent))]
    entries = entries.at[tuple(spot)].set(low)
    longest = extent.index(max(extent))
    spot[longest] = (spot[longest] + 1) % extent[longest]
    return entries.at[tuple(spot)].set(largest)


def steps_of(stream_key, extent, pieces, least, largest):
    loudness = 1.0
    for axis_at, blocks in pieces:
        steps = jax.random.uniform(jax.random.fold_in(jax.random.fold_in(stream_key, 6), axis_at), (blocks,), jnp.float32, least / len(pieces), largest / len(pieces))
        loudness = loudness * jnp.repeat(jnp.exp(steps), extent[axis_at] // blocks).reshape((-1,) + (1,) * (len(extent) - 1 - axis_at))
    return loudness


def scatter_about(rng, shape, deviation, limit, shards=(), kind=jnp.bfloat16):
    loudness = steps_of(rng, shape, shards, -0.22, 0.18) if shards else 1.0
    entries = jax.random.normal(rng, shape, jnp.float32) * deviation * loudness
    return jnp.minimum(jnp.maximum(entries, -limit), limit).astype(kind)


def setup_inputs(seed: int = 0) -> dict:
    key_of = jax.random.split(jax.random.key(seed), 8)
    observed = scatter_about(key_of[0], (NRAY, CH), 1.0, 6.0, ((0, 32),), jnp.float32)
    ray_start = set_ends(jax.random.randint(key_of[1], (NRAY,), 0, NT), jax.random.fold_in(key_of[1], 1), 0, NT - 1).astype(jnp.int32)
    tile_cells = draw_tile_cells(jax.random.fold_in(key_of[7], 71), 0)
    tile_lengths = jnp.clip(0.05 + 0.15 * jax.random.uniform(key_of[3], (NRAY * SPAN, TILE), jnp.float32) ** steps_of(key_of[3], (NRAY * SPAN, TILE), ((0, 32),), -0.2, 0.2), 0.05, 0.2)
    channel_kernel = scatter_about(key_of[4], (S, CH), CH ** -0.5, 0.75, (), jnp.float32)
    noise_weight = jnp.clip(jnp.exp(jax.random.uniform(key_of[5], (CH,), jnp.float32, math.log(0.25), math.log(4.0))), 0.25, 4.0)
    prior_weight = jnp.clip(jnp.exp(jax.random.uniform(key_of[6], (S,), jnp.float32, math.log(0.05), math.log(0.5))), 0.05, 0.5)
    return dict(observed=observed, ray_start=ray_start, tile_cells=tile_cells, tile_lengths=tile_lengths, channel_kernel=channel_kernel, noise_weight=noise_weight, prior_weight=prior_weight)


highest = lax.Precision.HIGHEST


def reference(observed, ray_start, tile_cells, tile_lengths, channel_kernel, noise_weight, prior_weight):
    reach = NT - 1
    span = 2 * NT - 1
    cell_count = CLON * CLAT * LEV
    weighted = channel_kernel * noise_weight[None, :]
    channel_gram = jnp.dot(weighted, channel_kernel.T, precision=highest)
    cell_table = tile_cells.reshape(N_ORBIT, N_LON, N_LAT, span, RAY_DEV, TILE)
    length_table = tile_lengths.reshape(N_ORBIT, N_LON, N_LAT, span, RAY_DEV, TILE)
    starts = ray_start.reshape(N_ORBIT, N_LON, N_LAT, RAY_DEV)
    lon_ids = jnp.arange(N_LON, dtype=jnp.int32)[:, None]
    lat_ids = jnp.arange(N_LAT, dtype=jnp.int32)[None, :]
    block_base = ((lon_ids * N_LAT + lat_ids) * cell_count).astype(jnp.int32)
    places = [(block_base[None, :, :, None, None] + cell_table[:, :, :, slot]).astype(jnp.int32) for slot in range(span)]
    lengths = [length_table[:, :, :, slot] for slot in range(span)]
    present = [((starts <= slot) & (starts + reach >= slot)).astype(jnp.float32) for slot in range(span)]
    ray_shape = (S, N_ORBIT, N_LON, N_LAT, RAY_DEV)

    def project(flat_field):
        total = jnp.zeros(ray_shape, jnp.float32)
        for slot in range(span):
            sums = jnp.sum(flat_field[:, places[slot]] * lengths[slot][None], axis=-1)
            sums = jnp.roll(sums, -(slot - reach), axis=2)
            total = total + sums * present[slot][None]
        return total

    def back(ray_image):
        summed = jnp.zeros((S, N_LON * N_LAT * cell_count), jnp.float32)
        for slot in range(span):
            moved = jnp.roll(ray_image * present[slot][None], slot - reach, axis=2)
            amounts = moved[..., None] * lengths[slot][None]
            summed = summed.at[:, places[slot].reshape(-1)].add(amounts.reshape(S, -1))
        return summed

    def to_grid(flat_field):
        shaped = flat_field.reshape(S, N_LON, N_LAT, CLON, CLAT, LEV).transpose(0, 1, 3, 2, 4, 5)
        return shaped.reshape(S, NLON, NLAT, LEV)

    def to_flat(field_value):
        shaped = field_value.reshape(S, N_LON, CLON, N_LAT, CLAT, LEV).transpose(0, 1, 3, 2, 4, 5)
        return shaped.reshape(S, N_LON * N_LAT * cell_count)

    def prior(field_value):
        padded = jnp.pad(field_value, ((0, 0), (0, 0), (1, 1), (1, 1)))
        neighbours = jnp.roll(field_value, 1, axis=1) + jnp.roll(field_value, -1, axis=1)
        neighbours = neighbours + padded[:, :, 2:, 1:-1] + padded[:, :, :-2, 1:-1]
        neighbours = neighbours + padded[:, :, 1:-1, 2:] + padded[:, :, 1:-1, :-2]
        return prior_weight[:, None, None, None] * (6.0 * field_value - neighbours)

    def operate(field_value):
        projected = project(to_flat(field_value))
        ray_image = jnp.dot(channel_gram, projected.reshape(S, -1), precision=highest).reshape(ray_shape)
        return to_grid(back(ray_image)) + prior(field_value)

    ray_source = lax.dot_general(weighted, observed, (((1,), (1,)), ((), ())), precision=highest)
    right_side = to_grid(back(ray_source.reshape(ray_shape)))
    solution_field = jnp.zeros_like(right_side)
    residual = right_side
    direction = right_side
    norm_now = jnp.sum(residual * residual)
    for turn_index in range(ITERS):
        image_field = operate(direction)
        step_size = norm_now / jnp.sum(direction * image_field)
        solution_field = solution_field + step_size * direction
        residual = residual - step_size * image_field
        norm_next = jnp.sum(residual * residual)
        direction = residual + (norm_next / norm_now) * direction
        norm_now = norm_next
    return solution_field, residual
```

```python
import functools

import jax
import jax.numpy as jnp
from jax import lax
from jax.experimental import pallas as pl
from jax.experimental.pallas import tpu as pltpu
from jax.sharding import PartitionSpec as P

CLON = 4
CLAT = 8
LEV = 128
NT = 3
ITERS = 4
SUB = 8
HALF = 256

highest = lax.Precision.HIGHEST
MESH = pl.DeviceIdType.MESH
f32 = jnp.float32
bf16 = jnp.bfloat16
NT_DIMS = (((1,), (1,)), ((), ()))


def each(count, step):
    if count <= 16:
        for k in range(count):
            step(k)
    else:
        lax.fori_loop(0, count, lambda k, c: (step(k), c)[1], 0)


def residues(reach, size):
    found = []
    for d in range(-reach, reach + 1):
        if d % size not in found:
            found.append(d % size)
    found.remove(0)
    return [0] + found


def kernel(sizes, observed, starts, cells, lengths, channel, noise, prior, x_out, r_out,
           ck8, gcol, pw, tab, w_hi, w_lo, latkey, source, ops, lon_halo, lat_halo,
           t_send, t_recv, d_recv, prior_acc, vec_x, vec_r, vec_w, vec_d, vec_s, vec_z,
           source_ssem, source_rsem, tab_ssem, tab_rsem, halo_ssem, halo_rsem,
           t_ssem, t_rsem, d_ssem, d_rsem):
    n_orbit, n_lon, n_lat = sizes
    reach = NT - 1
    span = 2 * NT - 1
    species, channels = channel.shape
    rays = starts.shape[1]
    tile = cells.shape[0]
    groups = residues(reach, n_lon)
    peers = residues(2 * reach, n_lon)
    group_of = [groups.index((u - reach) % n_lon) for u in range(span)]
    planes = n_lon * n_lat
    orbit = lax.axis_index("orbit")
    lon = lax.axis_index("lon")
    lat = lax.axis_index("lat")
    place = lon * n_lat + lat

    barrier = pltpu.get_barrier_semaphore()

    def plane_peer(k):
        there = lax.rem(place + k, planes)
        return (orbit, there // n_lat, lax.rem(there, n_lat))

    def greet(k):
        pl.semaphore_signal(barrier, inc=1, device_id=plane_peer(k + 1), device_id_type=MESH)

    each(planes - 1, greet)
    for o in range(1, n_orbit):
        for d in groups:
            pl.semaphore_signal(
                barrier, inc=1, device_id_type=MESH,
                device_id=(lax.rem(orbit + o, n_orbit), lax.rem(lon + d, n_lon), lat))

    ck8[...] = jnp.zeros_like(ck8)
    ck8[0:species, :] = channel[...]
    kernel_rows = ck8[...]
    weighted = kernel_rows * noise[...]
    gram = lax.dot_general(weighted, kernel_rows, NT_DIMS, precision=highest,
                           preferred_element_type=f32)
    for t in range(species):
        gcol[t] = jnp.broadcast_to(gram[:, t:t + 1], (SUB, LEV))
    sublane = lax.broadcasted_iota(jnp.int32, (SUB, LEV), 0)
    own_source = jnp.dot(weighted, observed[...], precision=highest, preferred_element_type=f32)
    source[orbit, 0] = jnp.where(sublane == species, starts[...].astype(f32), own_source)
    diagonal = (lax.broadcasted_iota(jnp.int32, (SUB, species), 0)
                == lax.broadcasted_iota(jnp.int32, (SUB, species), 1))
    pw_col = jnp.sum(jnp.where(diagonal, prior[...], 0.0), axis=1, keepdims=True)
    pw[...] = jnp.broadcast_to(pw_col, (SUB, LEV))

    own_cells = cells[...]
    own_lengths = lengths[...]
    totals = jnp.zeros_like(own_lengths)
    for m in range(tile):
        totals = totals + jnp.where(own_cells == own_cells[m:m + 1, :], own_lengths[m:m + 1, :], 0.0)
    tab[orbit, 0:tile, :] = own_cells.astype(f32)
    tab[orbit, tile:2 * tile, :] = totals

    pl.semaphore_wait(barrier, planes - 1 + (n_orbit - 1) * len(groups))

    tab_copies = []
    for o in range(1, n_orbit):
        copy = pltpu.make_async_remote_copy(
            src_ref=tab.at[orbit], dst_ref=tab.at[orbit],
            send_sem=tab_ssem.at[o], recv_sem=tab_rsem.at[o],
            device_id=(lax.rem(orbit + o, n_orbit), lon, lat), device_id_type=MESH)
        copy.start()
        tab_copies.append(copy)
    source_copies = []
    for o in range(n_orbit):
        for g, d in enumerate(groups):
            if o == 0 and g == 0:
                continue
            copy = pltpu.make_async_remote_copy(
                src_ref=source.at[orbit, 0], dst_ref=source.at[orbit, g],
                send_sem=source_ssem.at[o, g], recv_sem=source_rsem.at[o, g],
                device_id=(lax.rem(orbit + o, n_orbit), lax.rem(lon + d, n_lon), lat),
                device_id_type=MESH)
            copy.start()
            source_copies.append(copy)

    def build(slot):
        def chunk(c, carry):
            at = pl.ds(pl.multiple_of(c * LEV, LEV), LEV)
            cell = tab[slot, 0:tile, at].astype(jnp.int32)
            key = (cell // (CLAT * LEV)) * LEV + lax.rem(cell, LEV)
            total = tab[slot, tile:2 * tile, at]
            hi = total.astype(bf16).astype(f32)
            lo = total - hi
            rows = (lax.broadcasted_iota(jnp.int32, (HALF // 16, 16, LEV), 0) * 16
                    + lax.broadcasted_iota(jnp.int32, (HALF // 16, 16, LEV), 1))
            rows = rows.astype(f32).astype(bf16)
            for half in range(CLON * LEV // HALF):
                acc_hi = jnp.zeros((HALF // 16, 16, LEV), bf16)
                acc_lo = jnp.zeros((HALF // 16, 16, LEV), bf16)
                near = (key - half * HALF).astype(f32)
                for m in range(tile):
                    wide = lambda v: jnp.broadcast_to(v[m:m + 1, :], (16, LEV)).astype(bf16)[None]
                    hit = rows == wide(near)
                    acc_hi = jnp.where(hit, wide(hi), acc_hi)
                    acc_lo = jnp.where(hit, wide(lo), acc_lo)
                w_hi[slot, half * HALF:(half + 1) * HALF, at] = acc_hi.reshape(HALF, LEV)
                w_lo[slot, half * HALF:(half + 1) * HALF, at] = acc_lo.reshape(HALF, LEV)
            return carry

        lax.fori_loop(0, span * rays // LEV, chunk, 0)

    build(orbit)
    for o in range(1, n_orbit):
        tab_copies[o - 1].wait()
        build(lax.rem(orbit + n_orbit - o, n_orbit))
    for copy in source_copies:
        copy.wait()

    for o in range(n_orbit):
        for u in range(span):
            first = source[o, group_of[u], species:species + 1, :].astype(jnp.int32)
            cell = tab[o, 0:1, u * rays:(u + 1) * rays].astype(jnp.int32)
            band = lax.rem(cell // LEV, CLAT)
            band = jnp.where((first <= u) & (first + reach >= u), band, -1)
            latkey[o, :, u * rays:(u + 1) * rays] = jnp.broadcast_to(band, (SUB, rays))

    def back(images):
        total = None
        for o in range(n_orbit):
            y = jnp.concatenate([images[o][group_of[u]] for u in range(span)], axis=1)
            y_hi = y.astype(bf16).astype(f32)
            y_lo = y - y_hi
            band = latkey[o]
            high = jnp.concatenate([jnp.where(band == b, y_hi, 0.0) for b in range(CLAT)], axis=0)
            low = jnp.concatenate([jnp.where(band == b, y_lo, 0.0) for b in range(CLAT)], axis=0)
            high = high.astype(bf16)
            both = jnp.concatenate([high, low.astype(bf16)], axis=0)
            first = lax.dot_general(both, w_hi[o], NT_DIMS, preferred_element_type=f32)
            second = lax.dot_general(high, w_lo[o], NT_DIMS, preferred_element_type=f32)
            rows = CLAT * SUB
            part = first[0:rows] + (first[rows:] + second)
            total = part if total is None else total + part
        return total

    def product(turn):
        v_ref = ops.at[turn]
        copies = []
        last = (CLON - 1) * LEV
        for side, (src, dst, device) in enumerate((
            (v_ref.at[:, last:last + LEV], lon_halo.at[turn, 0], (orbit, lax.rem(lon + 1, n_lon), lat)),
            (v_ref.at[:, 0:LEV], lon_halo.at[turn, 1], (orbit, lax.rem(lon + n_lon - 1, n_lon), lat)),
            (v_ref.at[(CLAT - 1) * SUB:CLAT * SUB, :], lat_halo.at[turn, 0], (orbit, lon, lax.rem(lat + 1, n_lat))),
            (v_ref.at[0:SUB, :], lat_halo.at[turn, 1], (orbit, lon, lax.rem(lat + n_lat - 1, n_lat))),
        )):
            copy = pltpu.make_async_remote_copy(
                src_ref=src, dst_ref=dst, send_sem=halo_ssem.at[turn, side],
                recv_sem=halo_rsem.at[turn, side], device_id=device, device_id_type=MESH)
            copy.start()
            copies.append(copy)
        v = v_ref[...]
        rows = CLAT * SUB
        v_high = v.astype(bf16)
        v_both = jnp.concatenate([v_high, (v - v_high.astype(f32)).astype(bf16)], axis=0)
        for o in range(n_orbit):
            first = jnp.dot(v_both, w_hi[o], preferred_element_type=f32)
            second = jnp.dot(v_high, w_lo[o], preferred_element_type=f32)
            sums = first[0:rows] + (first[rows:] + second)
            band = latkey[o]
            picked = jnp.zeros((SUB, span * rays), f32)
            for b in range(CLAT):
                picked = jnp.where(band == b, sums[b * SUB:(b + 1) * SUB], picked)
            for g in range(len(groups)):
                mine = [picked[:, u * rays:(u + 1) * rays] for u in range(span) if group_of[u] == g]
                t_send[turn, o * len(groups) + g] = functools.reduce(lambda a, b: a + b, mine)
        t_copies = []
        for k, distance in enumerate(peers):
            if k == 0:
                continue
            copy = pltpu.make_async_remote_copy(
                src_ref=t_send.at[turn], dst_ref=t_recv.at[turn, k - 1],
                send_sem=t_ssem.at[turn, k], recv_sem=t_rsem.at[turn, k],
                device_id=(orbit, lax.rem(lon + distance, n_lon), lat), device_id_type=MESH)
            copy.start()
            t_copies.append(copy)

        for copy in copies:
            copy.wait()
        lane = lax.broadcasted_iota(jnp.int32, (rows, LEV), 1)
        weight = jnp.concatenate([pw[...]] * CLAT, axis=0)
        column = lambda c: v_ref[:, c * LEV:(c + 1) * LEV]
        for c in range(CLON):
            here = column(c)
            south = jnp.where(lat == 0, 0.0, lat_halo[turn, 0, :, c * LEV:(c + 1) * LEV])
            north = jnp.where(lat == n_lat - 1, 0.0, lat_halo[turn, 1, :, c * LEV:(c + 1) * LEV])
            around = column(c - 1) if c > 0 else lon_halo[turn, 0]
            around = around + (column(c + 1) if c < CLON - 1 else lon_halo[turn, 1])
            around = around + jnp.concatenate([south, here[:-SUB]], axis=0)
            around = around + jnp.concatenate([here[SUB:], north], axis=0)
            around = around + jnp.where(lane == 0, 0.0, pltpu.roll(here, 1, 1))
            around = around + jnp.where(lane == LEV - 1, 0.0, pltpu.roll(here, LEV - 1, 1))
            prior_acc[:, c * LEV:(c + 1) * LEV] = weight * (6.0 * here - around)

        for copy in t_copies:
            copy.wait()
        images = []
        for o in range(n_orbit):
            per_group = []
            for g, d in enumerate(groups):
                total = t_send[turn, o * len(groups) + g]
                for k, distance in enumerate(peers):
                    theirs = (d - distance) % n_lon
                    if k > 0 and theirs in groups:
                        total = total + t_recv[turn, k - 1, o * len(groups) + groups.index(theirs)]
                image = jnp.zeros((SUB, rays), f32)
                for t in range(species):
                    image = image + gcol[t] * total[t:t + 1, :]
                per_group.append(image)
            images.append(per_group)
        return back(images) + prior_acc[...]

    def inner(a, b):
        whole = a * b
        lanes = sum(whole[:, c * LEV:(c + 1) * LEV] for c in range(CLON))
        return jnp.sum(lanes, axis=0, keepdims=True)

    def start_dots(turn):
        r = vec_r[...]
        w = vec_w[...]
        terms = [inner(r, r), inner(r, w)]
        if turn > 0:
            terms += [inner(r, vec_s[...]), inner(vec_d[...], w)]
        terms.append(jnp.zeros((SUB - len(terms), LEV), f32))
        d_recv[turn, 0] = jnp.concatenate(terms, axis=0)

        def send(k):
            pltpu.make_async_remote_copy(
                src_ref=d_recv.at[turn, 0], dst_ref=d_recv.at[turn, k + 1],
                send_sem=d_ssem.at[turn], recv_sem=d_rsem.at[turn],
                device_id=plane_peer(k + 1), device_id_type=MESH).start()

        each(planes - 1, send)

    def finish_dots(turn):
        pltpu.make_async_remote_copy(
            src_ref=d_recv.at[turn, pl.ds(1, planes - 1)], dst_ref=d_recv.at[turn, pl.ds(1, planes - 1)],
            send_sem=d_ssem.at[turn], recv_sem=d_rsem.at[turn],
            device_id=plane_peer(1), device_id_type=MESH).wait()
        total = jnp.zeros((SUB, LEV), f32)
        for f in range(planes):
            total = total + d_recv[turn, lax.rem(place + planes - f, planes)]
        sums = jnp.sum(total, axis=1, keepdims=True)
        return [sums[i:i + 1, :] for i in range(4)]

    images = [[jnp.where(sublane < species, source[o, g], 0.0) for g in range(len(groups))]
              for o in range(n_orbit)]
    right_side = back(images)
    vec_r[...] = right_side
    ops[0] = right_side
    vec_w[...] = product(0)
    norm_before = None
    curvature = None
    for turn in range(ITERS):
        start_dots(turn)
        more = turn < ITERS - 1
        if more:
            ops[turn + 1] = vec_w[...]
            image = product(turn + 1)
        norm, cross, cross_s, cross_d = finish_dots(turn)
        if turn == 0:
            curvature = cross
            alpha = norm / curvature
            direction = vec_r[...]
            moved = vec_w[...]
            vec_x[...] = alpha * direction
            if more:
                twice = image
        else:
            beta = norm / norm_before
            curvature = cross + beta * (cross_s + cross_d) + beta * beta * curvature
            alpha = norm / curvature
            direction = vec_r[...] + beta * vec_d[...]
            moved = vec_w[...] + beta * vec_s[...]
            vec_x[...] = vec_x[...] + alpha * direction
            if more:
                twice = image + beta * vec_z[...]
        vec_r[...] = vec_r[...] - alpha * moved
        if more:
            vec_d[...] = direction
            vec_s[...] = moved
            vec_z[...] = twice
            vec_w[...] = vec_w[...] - alpha * twice
        norm_before = norm
    x_out[...] = vec_x[...]
    r_out[...] = vec_r[...]


def body(sizes, observed, ray_start, tile_cells, tile_lengths, channel_kernel, noise_weight, prior_weight):
    n_orbit, n_lon, n_lat = sizes
    species, channels = channel_kernel.shape
    rays = ray_start.shape[0]
    rows, tile = tile_cells.shape
    groups = len(residues(NT - 1, n_lon))
    peers = len(residues(2 * (NT - 1), n_lon))
    flat = (CLAT * SUB, CLON * LEV)
    vmem = pltpu.VMEM
    dma = pltpu.SemaphoreType.DMA
    out = jax.ShapeDtypeStruct(flat, f32)
    solved, left = pl.pallas_call(
        functools.partial(kernel, sizes),
        out_shape=(out, out),
        in_specs=[pl.BlockSpec(memory_space=pltpu.VMEM)] * 7,
        out_specs=[pl.BlockSpec(memory_space=pltpu.VMEM)] * 2,
        scratch_shapes=[
            vmem((SUB, channels), f32),
            vmem((species, SUB, LEV), f32),
            vmem((SUB, LEV), f32),
            vmem((n_orbit, 2 * tile, rows), f32),
            vmem((n_orbit, CLON * LEV, rows), bf16),
            vmem((n_orbit, CLON * LEV, rows), bf16),
            vmem((n_orbit, SUB, rows), jnp.int32),
            vmem((n_orbit, groups, SUB, rays), f32),
            vmem((ITERS,) + flat, f32),
            vmem((ITERS, 2, flat[0], LEV), f32),
            vmem((ITERS, 2, SUB, flat[1]), f32),
            vmem((ITERS, n_orbit * groups, SUB, rays), f32),
            vmem((ITERS, peers - 1, n_orbit * groups, SUB, rays), f32),
            vmem((ITERS, n_lon * n_lat, SUB, LEV), f32),
        ] + [vmem(flat, f32)] * 7 + [
            dma((n_orbit, groups)), dma((n_orbit, groups)),
            dma((n_orbit,)), dma((n_orbit,)),
            dma((ITERS, 4)), dma((ITERS, 4)),
            dma((ITERS, peers)), dma((ITERS, peers)),
            dma((ITERS,)), dma((ITERS,)),
        ],
        compiler_params=pltpu.CompilerParams(
            collective_id=0, has_side_effects=True, vmem_limit_bytes=40 * 1024 * 1024),
    )(
        observed.T, ray_start.reshape(1, rays), tile_cells.T, tile_lengths.T,
        channel_kernel, noise_weight.reshape(1, channels), prior_weight.reshape(1, species),
    )

    def placed(field):
        shaped = field.reshape(CLAT, SUB, CLON, LEV)[:, :species]
        return shaped.transpose(1, 2, 0, 3)

    return placed(solved), placed(left)


def solution(mesh):
    sizes = tuple(mesh.shape[name] for name in ("orbit", "lon", "lat"))
    return jax.shard_map(
        functools.partial(body, sizes),
        mesh=mesh,
        in_specs=(
            P(("orbit", "lon", "lat"), None),
            P(("orbit", "lon", "lat")),
            P(("orbit", "lon", "lat"), None),
            P(("orbit", "lon", "lat"), None),
            P(),
            P(),
            P(),
        ),
        out_specs=(P(None, "lon", "lat", None), P(None, "lon", "lat", None)),
        check_vma=False,
    )
```

```python
import functools

import jax
import jax.numpy as jnp
from jax import lax
from jax.experimental import pallas as pl
from jax.experimental.pallas import tpu as pltpu
from jax.sharding import PartitionSpec as P

CLON = 4
CLAT = 8
LEV = 128
NT = 3
ITERS = 4
SUB = 8
HALF = 256

highest = lax.Precision.HIGHEST
MESH = pl.DeviceIdType.MESH
f32 = jnp.float32
bf16 = jnp.bfloat16
NT_DIMS = (((1,), (1,)), ((), ()))


def each(count, step):
    if count <= 16:
        for k in range(count):
            step(k)
    else:
        lax.fori_loop(0, count, lambda k, c: (step(k), c)[1], 0)


def residues(reach, size):
    found = []
    for d in range(-reach, reach + 1):
        if d % size not in found:
            found.append(d % size)
    found.remove(0)
    return [0] + found


def kernel(sizes, observed_in, starts_in, cells_in, lengths_in, channel_in, noise_in, prior_in,
           x_out, r_out, observed, starts, cells, lengths, channel, noise, prior, load_sem,
           ck8, gcol, pw, tab, w_hi, w_lo, latkey, source, ops, lon_halo, lat_halo,
           t_send, t_recv, d_recv, prior_acc, vec_x, vec_r, vec_w, vec_d, vec_s, vec_z,
           source_ssem, source_rsem, tab_ssem, tab_rsem, halo_ssem, halo_rsem,
           t_ssem, t_rsem, d_ssem, d_rsem):
    n_orbit, n_lon, n_lat = sizes
    reach = NT - 1
    span = 2 * NT - 1
    species, channels = channel.shape
    rays = starts.shape[1]
    tile = cells.shape[0]
    groups = residues(reach, n_lon)
    peers = residues(2 * reach, n_lon)
    group_of = [groups.index((u - reach) % n_lon) for u in range(span)]
    planes = n_lon * n_lat
    orbit = lax.axis_index("orbit")
    lon = lax.axis_index("lon")
    lat = lax.axis_index("lat")
    place = lon * n_lat + lat

    barrier = pltpu.get_barrier_semaphore()
    loads = [
        pltpu.make_async_copy(src, dst, load_sem.at[i])
        for i, (src, dst) in enumerate((
            (cells_in, cells), (lengths_in, lengths), (observed_in, observed), (channel_in, channel),
            (noise_in, noise), (starts_in, starts), (prior_in, prior)))
    ]
    for load in loads:
        load.start()

    def plane_peer(k):
        there = lax.rem(place + k, planes)
        return (orbit, lax.div(there, n_lat), lax.rem(there, n_lat))

    def greet(k):
        pl.semaphore_signal(barrier, inc=1, device_id=plane_peer(k + 1), device_id_type=MESH)

    each(planes - 1, greet)
    for o in range(1, n_orbit):
        for d in groups:
            pl.semaphore_signal(
                barrier, inc=1, device_id_type=MESH,
                device_id=(lax.rem(orbit + o, n_orbit), lax.rem(lon + d, n_lon), lat))

    for load in loads[:2]:
        load.wait()
    own_cells = cells[...]
    own_lengths = lengths[...]
    totals = jnp.zeros_like(own_lengths)
    for m in range(tile):
        totals = totals + jnp.where(own_cells == own_cells[m:m + 1, :], own_lengths[m:m + 1, :], 0.0)
    tab[orbit, 0:tile, :] = own_cells.astype(f32)
    tab[orbit, tile:2 * tile, :] = totals

    pl.semaphore_wait(barrier, planes - 1 + (n_orbit - 1) * len(groups))

    tab_copies = []
    for o in range(1, n_orbit):
        copy = pltpu.make_async_remote_copy(
            src_ref=tab.at[orbit], dst_ref=tab.at[orbit],
            send_sem=tab_ssem.at[o], recv_sem=tab_rsem.at[o],
            device_id=(lax.rem(orbit + o, n_orbit), lon, lat), device_id_type=MESH)
        copy.start()
        tab_copies.append(copy)
    for load in loads[2:]:
        load.wait()
    ck8[...] = jnp.zeros_like(ck8)
    ck8[0:species, :] = channel[...]
    kernel_rows = ck8[...]
    weighted = kernel_rows * noise[...]
    sublane = lax.broadcasted_iota(jnp.int32, (SUB, LEV), 0)
    own_source = jnp.dot(weighted, observed[...], precision=highest, preferred_element_type=f32)
    source[orbit, 0] = jnp.where(sublane == species, starts[...].astype(f32), own_source)
    source_copies = []
    for o in range(n_orbit):
        for g, d in enumerate(groups):
            if o == 0 and g == 0:
                continue
            copy = pltpu.make_async_remote_copy(
                src_ref=source.at[orbit, 0], dst_ref=source.at[orbit, g],
                send_sem=source_ssem.at[o, g], recv_sem=source_rsem.at[o, g],
                device_id=(lax.rem(orbit + o, n_orbit), lax.rem(lon + d, n_lon), lat),
                device_id_type=MESH)
            copy.start()
            source_copies.append(copy)

    gram = lax.dot_general(weighted, kernel_rows, NT_DIMS, precision=highest,
                           preferred_element_type=f32)
    for t in range(species):
        gcol[t] = jnp.broadcast_to(gram[:, t:t + 1], (SUB, LEV))
    diagonal = (lax.broadcasted_iota(jnp.int32, (SUB, species), 0)
                == lax.broadcasted_iota(jnp.int32, (SUB, species), 1))
    pw_col = jnp.sum(jnp.where(diagonal, prior[...], 0.0), axis=1, keepdims=True)
    pw[...] = jnp.broadcast_to(pw_col, (SUB, LEV))

    def build(slot):
        def chunk(c, carry):
            at = pl.ds(pl.multiple_of(c * LEV, LEV), LEV)
            cell = tab[slot, 0:tile, at].astype(jnp.int32)
            key = (cell // (CLAT * LEV)) * LEV + lax.rem(cell, LEV)
            total = tab[slot, tile:2 * tile, at]
            hi = total.astype(bf16).astype(f32)
            lo = total - hi
            rows = (lax.broadcasted_iota(jnp.int32, (HALF // 16, 16, LEV), 0) * 16
                    + lax.broadcasted_iota(jnp.int32, (HALF // 16, 16, LEV), 1))
            rows = rows.astype(f32).astype(bf16)
            for half in range(CLON * LEV // HALF):
                acc_hi = jnp.zeros((HALF // 16, 16, LEV), bf16)
                acc_lo = jnp.zeros((HALF // 16, 16, LEV), bf16)
                near = (key - half * HALF).astype(f32)
                for m in range(tile):
                    wide = lambda v: jnp.broadcast_to(v[m:m + 1, :], (16, LEV)).astype(bf16)[None]
                    hit = rows == wide(near)
                    acc_hi = jnp.where(hit, wide(hi), acc_hi)
                    acc_lo = jnp.where(hit, wide(lo), acc_lo)
                w_hi[slot, half * HALF:(half + 1) * HALF, at] = acc_hi.reshape(HALF, LEV)
                w_lo[slot, half * HALF:(half + 1) * HALF, at] = acc_lo.reshape(HALF, LEV)
            return carry

        lax.fori_loop(0, span * rays // LEV, chunk, 0)

    build(orbit)
    for o in range(1, n_orbit):
        tab_copies[o - 1].wait()
        build(lax.rem(orbit + n_orbit - o, n_orbit))
    for copy in source_copies:
        copy.wait()

    for o in range(n_orbit):
        for u in range(span):
            first = source[o, group_of[u], species:species + 1, :].astype(jnp.int32)
            cell = tab[o, 0:1, u * rays:(u + 1) * rays].astype(jnp.int32)
            band = lax.rem(cell // LEV, CLAT)
            band = jnp.where((first <= u) & (first + reach >= u), band, -1)
            latkey[o, :, u * rays:(u + 1) * rays] = jnp.broadcast_to(band, (SUB, rays))

    def back(images):
        total = None
        for o in range(n_orbit):
            part = back_orbit(o, images[o])
            total = part if total is None else total + part
        return total

    def back_orbit(o, per_group):
        y = jnp.concatenate([per_group[group_of[u]] for u in range(span)], axis=1)
        y_hi = y.astype(bf16).astype(f32)
        y_lo = y - y_hi
        band = latkey[o]
        high = jnp.concatenate([jnp.where(band == b, y_hi, 0.0) for b in range(CLAT)], axis=0)
        low = jnp.concatenate([jnp.where(band == b, y_lo, 0.0) for b in range(CLAT)], axis=0)
        high = high.astype(bf16)
        both = jnp.concatenate([high, low.astype(bf16)], axis=0)
        first = lax.dot_general(both, w_hi[o], NT_DIMS, preferred_element_type=f32)
        second = lax.dot_general(high, w_lo[o], NT_DIMS, preferred_element_type=f32)
        rows = CLAT * SUB
        return first[0:rows] + (first[rows:] + second)

    def product(turn, send_sums=None, between=None):
        v_ref = ops.at[turn]
        copies = []
        last = (CLON - 1) * LEV
        for side, (src, dst, device) in enumerate((
            (v_ref.at[:, last:last + LEV], lon_halo.at[turn, 0], (orbit, lax.rem(lon + 1, n_lon), lat)),
            (v_ref.at[:, 0:LEV], lon_halo.at[turn, 1], (orbit, lax.rem(lon + n_lon - 1, n_lon), lat)),
            (v_ref.at[(CLAT - 1) * SUB:CLAT * SUB, :], lat_halo.at[turn, 0], (orbit, lon, lax.rem(lat + 1, n_lat))),
            (v_ref.at[0:SUB, :], lat_halo.at[turn, 1], (orbit, lon, lax.rem(lat + n_lat - 1, n_lat))),
        )):
            copy = pltpu.make_async_remote_copy(
                src_ref=src, dst_ref=dst, send_sem=halo_ssem.at[turn, side],
                recv_sem=halo_rsem.at[turn, side], device_id=device, device_id_type=MESH)
            copy.start()
            copies.append(copy)
        v = v_ref[...]
        rows = CLAT * SUB
        v_high = v.astype(bf16)
        t_copies = [[] for _ in range(n_orbit)]
        v_both = jnp.concatenate([v_high, (v - v_high.astype(f32)).astype(bf16)], axis=0)
        for o in range(n_orbit):
            first = jnp.dot(v_both, w_hi[o], preferred_element_type=f32)
            second = jnp.dot(v_high, w_lo[o], preferred_element_type=f32)
            sums = first[0:rows] + (first[rows:] + second)
            band = latkey[o]
            picked = jnp.zeros((SUB, span * rays), f32)
            for b in range(CLAT):
                picked = jnp.where(band == b, sums[b * SUB:(b + 1) * SUB], picked)
            for g in range(len(groups)):
                mine = [picked[:, u * rays:(u + 1) * rays] for u in range(span) if group_of[u] == g]
                t_send[turn, o, g] = functools.reduce(lambda a, b: a + b, mine)
            for k, distance in enumerate(peers):
                if k == 0:
                    continue
                copy = pltpu.make_async_remote_copy(
                    src_ref=t_send.at[turn, o], dst_ref=t_recv.at[turn, k - 1, o],
                    send_sem=t_ssem.at[turn, k, o], recv_sem=t_rsem.at[turn, k, o],
                    device_id=(orbit, lax.rem(lon + distance, n_lon), lat), device_id_type=MESH)
                copy.start()
                t_copies[o].append(copy)
            if o == 0 and send_sums is not None:
                send_sums()

        for copy in copies:
            copy.wait()
        lane = lax.broadcasted_iota(jnp.int32, (rows, LEV), 1)
        weight = jnp.concatenate([pw[...]] * CLAT, axis=0)
        column = lambda c: v_ref[:, c * LEV:(c + 1) * LEV]
        for c in range(CLON):
            here = column(c)
            south = jnp.where(lat == 0, 0.0, lat_halo[turn, 0, :, c * LEV:(c + 1) * LEV])
            north = jnp.where(lat == n_lat - 1, 0.0, lat_halo[turn, 1, :, c * LEV:(c + 1) * LEV])
            around = column(c - 1) if c > 0 else lon_halo[turn, 0]
            around = around + (column(c + 1) if c < CLON - 1 else lon_halo[turn, 1])
            around = around + jnp.concatenate([south, here[:-SUB]], axis=0)
            around = around + jnp.concatenate([here[SUB:], north], axis=0)
            around = around + jnp.where(lane == 0, 0.0, pltpu.roll(here, 1, 1))
            around = around + jnp.where(lane == LEV - 1, 0.0, pltpu.roll(here, LEV - 1, 1))
            prior_acc[:, c * LEV:(c + 1) * LEV] = weight * (6.0 * here - around)

        if between is not None:
            between()
        result = prior_acc[...]
        for o in range(n_orbit):
            for copy in t_copies[o]:
                copy.wait()
            per_group = []
            for g, d in enumerate(groups):
                total = t_send[turn, o, g]
                for k, distance in enumerate(peers):
                    theirs = (d - distance) % n_lon
                    if k > 0 and theirs in groups:
                        total = total + t_recv[turn, k - 1, o, groups.index(theirs)]
                image = jnp.zeros((SUB, rays), f32)
                for t in range(species):
                    image = image + gcol[t] * total[t:t + 1, :]
                per_group.append(image)
            result = result + back_orbit(o, per_group)
        return result

    def inner(a, b):
        whole = a * b
        lanes = sum(whole[:, c * LEV:(c + 1) * LEV] for c in range(CLON))
        return jnp.sum(jnp.sum(lanes, axis=0, keepdims=True), axis=1, keepdims=True)

    def form_dots(turn):
        r = vec_r[...]
        w = ops[turn + 1] if turn + 1 < ITERS else vec_w[...]
        terms = [inner(r, r), inner(r, w)]
        if turn > 0:
            terms += [inner(r, vec_s[...]), inner(vec_d[...], w)]
        spot = lax.broadcasted_iota(jnp.int32, (1, LEV), 1)
        row = jnp.zeros((1, LEV), f32)
        for i, term in enumerate(terms):
            row = jnp.where(spot == i, term, row)
        d_recv[turn, 0] = row

    def send_dots(turn):
        def send(k):
            pltpu.make_async_remote_copy(
                src_ref=d_recv.at[turn, 0], dst_ref=d_recv.at[turn, k + 1],
                send_sem=d_ssem.at[turn], recv_sem=d_rsem.at[turn],
                device_id=plane_peer(k + 1), device_id_type=MESH).start()

        each(planes - 1, send)

    def finish_dots(turn):
        pltpu.make_async_remote_copy(
            src_ref=d_recv.at[turn, pl.ds(1, planes - 1)], dst_ref=d_recv.at[turn, pl.ds(1, planes - 1)],
            send_sem=d_ssem.at[turn], recv_sem=d_rsem.at[turn],
            device_id=plane_peer(1), device_id_type=MESH).wait()
        total = jnp.zeros((1, LEV), f32)
        for f in range(planes):
            total = total + d_recv[turn, lax.rem(place + planes - f, planes)]
        return [total[:, i:i + 1] for i in range(4)]

    images = [[jnp.where(sublane < species, source[o, g], 0.0) for g in range(len(groups))]
              for o in range(n_orbit)]
    right_side = back(images)
    vec_r[...] = right_side
    ops[0] = right_side
    ops[1] = product(0)
    kept = {}

    def advance(turn):
        norm, cross, cross_s, cross_d = finish_dots(turn)
        w = ops[turn + 1] if turn + 1 < ITERS else vec_w[...]
        if turn == 0:
            kept["curvature"] = cross
            alpha = norm / cross
            direction = vec_r[...]
            moved = w
            vec_x[...] = alpha * direction
        else:
            beta = norm / kept["norm"]
            kept["beta"] = beta
            kept["curvature"] = cross + beta * (cross_s + cross_d) + beta * beta * kept["curvature"]
            alpha = norm / kept["curvature"]
            direction = vec_r[...] + beta * vec_d[...]
            moved = w + beta * vec_s[...]
            vec_x[...] = vec_x[...] + alpha * direction
        vec_r[...] = vec_r[...] - alpha * moved
        if turn < ITERS - 1:
            vec_d[...] = direction
            vec_s[...] = moved
        kept["norm"] = norm
        kept["alpha"] = alpha

    for turn in range(ITERS - 1):
        form_dots(turn)
        image = product(turn + 1, lambda: send_dots(turn), lambda: advance(turn))
        twice = image if turn == 0 else image + kept["beta"] * vec_z[...]
        vec_z[...] = twice
        moved_on = ops[turn + 1] - kept["alpha"] * twice
        if turn + 2 < ITERS:
            ops[turn + 2] = moved_on
        else:
            vec_w[...] = moved_on
    form_dots(ITERS - 1)
    send_dots(ITERS - 1)
    advance(ITERS - 1)
    x_out[...] = vec_x[...]
    r_out[...] = vec_r[...]


def body(sizes, observed, ray_start, tile_cells, tile_lengths, channel_kernel, noise_weight, prior_weight):
    n_orbit, n_lon, n_lat = sizes
    species, channels = channel_kernel.shape
    rays = ray_start.shape[0]
    rows, tile = tile_cells.shape
    groups = len(residues(NT - 1, n_lon))
    peers = len(residues(2 * (NT - 1), n_lon))
    flat = (CLAT * SUB, CLON * LEV)
    vmem = pltpu.VMEM
    dma = pltpu.SemaphoreType.DMA
    out = jax.ShapeDtypeStruct(flat, f32)
    solved, left = pl.pallas_call(
        functools.partial(kernel, sizes),
        out_shape=(out, out),
        in_specs=[pl.BlockSpec(memory_space=pltpu.HBM)] * 7,
        out_specs=[pl.BlockSpec(memory_space=pltpu.VMEM)] * 2,
        scratch_shapes=[
            vmem((channels, rays), f32),
            vmem((1, rays), jnp.int32),
            vmem((tile, rows), jnp.int32),
            vmem((tile, rows), f32),
            vmem((species, channels), f32),
            vmem((1, channels), f32),
            vmem((1, species), f32),
            dma((7,)),
            vmem((SUB, channels), f32),
            vmem((species, SUB, LEV), f32),
            vmem((SUB, LEV), f32),
            vmem((n_orbit, 2 * tile, rows), f32),
            vmem((n_orbit, CLON * LEV, rows), bf16),
            vmem((n_orbit, CLON * LEV, rows), bf16),
            vmem((n_orbit, SUB, rows), jnp.int32),
            vmem((n_orbit, groups, SUB, rays), f32),
            vmem((ITERS,) + flat, f32),
            vmem((ITERS, 2, flat[0], LEV), f32),
            vmem((ITERS, 2, SUB, flat[1]), f32),
            vmem((ITERS, n_orbit, groups, SUB, rays), f32),
            vmem((ITERS, peers - 1, n_orbit, groups, SUB, rays), f32),
            vmem((ITERS, n_lon * n_lat, 1, LEV), f32),
        ] + [vmem(flat, f32)] * 7 + [
            dma((n_orbit, groups)), dma((n_orbit, groups)),
            dma((n_orbit,)), dma((n_orbit,)),
            dma((ITERS, 4)), dma((ITERS, 4)),
            dma((ITERS, peers, n_orbit)), dma((ITERS, peers, n_orbit)),
            dma((ITERS,)), dma((ITERS,)),
        ],
        compiler_params=pltpu.CompilerParams(
            collective_id=0, has_side_effects=True, vmem_limit_bytes=40 * 1024 * 1024),
    )(
        observed.T, ray_start.reshape(1, rays), tile_cells.T, tile_lengths.T,
        channel_kernel, noise_weight.reshape(1, channels), prior_weight.reshape(1, species),
    )

    def placed(field):
        shaped = field.reshape(CLAT, SUB, CLON, LEV)[:, :species]
        return shaped.transpose(1, 2, 0, 3)

    return placed(solved), placed(left)


def solution(mesh):
    sizes = tuple(mesh.shape[name] for name in ("orbit", "lon", "lat"))
    return jax.shard_map(
        functools.partial(body, sizes),
        mesh=mesh,
        in_specs=(
            P(("orbit", "lon", "lat"), None),
            P(("orbit", "lon", "lat")),
            P(("orbit", "lon", "lat"), None),
            P(("orbit", "lon", "lat"), None),
            P(),
            P(),
            P(),
        ),
        out_specs=(P(None, "lon", "lat", None), P(None, "lon", "lat", None)),
        check_vma=False,
    )
```

```python
import functools

import jax
import jax.numpy as jnp
from jax import lax
from jax.experimental import pallas as pl
from jax.experimental.pallas import tpu as pltpu
from jax.sharding import PartitionSpec as P

CLON = 4
CLAT = 8
LEV = 128
NT = 3
ITERS = 4
SUB = 8
HALF = 256
VMEM_BYTES = 60 * 1024 * 1024

highest = lax.Precision.HIGHEST
MESH = pl.DeviceIdType.MESH
f32 = jnp.float32
bf16 = jnp.bfloat16
NT_DIMS = (((1,), (1,)), ((), ()))


def each(count, step):
    if count <= 16:
        for k in range(count):
            step(k)
    else:
        lax.fori_loop(0, count, lambda k, c: (step(k), c)[1], 0)


def residues(reach, size):
    found = []
    for d in range(-reach, reach + 1):
        if d % size not in found:
            found.append(d % size)
    found.remove(0)
    return [0] + found


def kernel(sizes, observed_in, starts_in, cells_in, lengths_in, channel_in, noise_in, prior_in,
           x_out, r_out, observed, starts, cells, lengths, channel, noise, prior, load_sem,
           ck8, gcol, pw, tab, w_hi, w_lo, latkey, source, ops, lon_halo, lat_halo,
           t_send, t_recv, d_recv, prior_acc, vec_x, vec_r, vec_w, vec_d, vec_s, vec_z,
           source_ssem, source_rsem, tab_ssem, tab_rsem, halo_ssem, halo_rsem,
           t_ssem, t_rsem, d_ssem, d_rsem):
    n_orbit, n_lon, n_lat = sizes
    reach = NT - 1
    span = 2 * NT - 1
    species, channels = channel.shape
    rays = starts.shape[1]
    tile = cells.shape[0]
    groups = residues(reach, n_lon)
    peers = residues(2 * reach, n_lon)
    group_of = [groups.index((u - reach) % n_lon) for u in range(span)]
    planes = n_lon * n_lat
    orbit = lax.axis_index("orbit")
    lon = lax.axis_index("lon")
    lat = lax.axis_index("lat")
    place = lon * n_lat + lat

    barrier = pltpu.get_barrier_semaphore()
    loads = [
        pltpu.make_async_copy(src, dst, load_sem.at[i])
        for i, (src, dst) in enumerate((
            (cells_in, cells), (lengths_in, lengths), (observed_in, observed), (channel_in, channel),
            (noise_in, noise), (starts_in, starts), (prior_in, prior)))
    ]
    for load in loads:
        load.start()

    def plane_peer(k):
        there = lax.rem(place + k, planes)
        return (orbit, lax.div(there, n_lat), lax.rem(there, n_lat))

    def greet(k):
        pl.semaphore_signal(barrier, inc=1, device_id=plane_peer(k + 1), device_id_type=MESH)

    each(planes - 1, greet)
    for o in range(1, n_orbit):
        for d in groups:
            pl.semaphore_signal(
                barrier, inc=1, device_id_type=MESH,
                device_id=(lax.rem(orbit + o, n_orbit), lax.rem(lon + d, n_lon), lat))

    for load in loads[:2]:
        load.wait()
    own_cells = cells[...]
    own_lengths = lengths[...]
    totals = jnp.zeros_like(own_lengths)
    for m in range(tile):
        totals = totals + jnp.where(own_cells == own_cells[m:m + 1, :], own_lengths[m:m + 1, :], 0.0)
    tab[orbit, 0:tile, :] = own_cells.astype(f32)
    tab[orbit, tile:2 * tile, :] = totals

    pl.semaphore_wait(barrier, planes - 1 + (n_orbit - 1) * len(groups))

    tab_copies = []
    for o in range(1, n_orbit):
        copy = pltpu.make_async_remote_copy(
            src_ref=tab.at[orbit], dst_ref=tab.at[orbit],
            send_sem=tab_ssem.at[o], recv_sem=tab_rsem.at[o],
            device_id=(lax.rem(orbit + o, n_orbit), lon, lat), device_id_type=MESH)
        copy.start()
        tab_copies.append(copy)
    for load in loads[2:]:
        load.wait()
    ck8[...] = jnp.zeros_like(ck8)
    ck8[0:species, :] = channel[...]
    kernel_rows = ck8[...]
    weighted = kernel_rows * noise[...]
    sublane = lax.broadcasted_iota(jnp.int32, (SUB, LEV), 0)
    own_source = jnp.dot(weighted, observed[...], precision=highest, preferred_element_type=f32)
    source[orbit, 0] = jnp.where(sublane == species, starts[...].astype(f32), own_source)
    source_copies = {}
    for o in range(n_orbit):
        for g, d in enumerate(groups):
            if o == 0 and g == 0:
                continue
            copy = pltpu.make_async_remote_copy(
                src_ref=source.at[orbit, 0], dst_ref=source.at[orbit, g],
                send_sem=source_ssem.at[o, g], recv_sem=source_rsem.at[o, g],
                device_id=(lax.rem(orbit + o, n_orbit), lax.rem(lon + d, n_lon), lat),
                device_id_type=MESH)
            copy.start()
            source_copies[(o, g)] = copy

    gram = lax.dot_general(weighted, kernel_rows, NT_DIMS, precision=highest,
                           preferred_element_type=f32)
    for t in range(species):
        gcol[t] = jnp.broadcast_to(gram[:, t:t + 1], (SUB, LEV))
    diagonal = (lax.broadcasted_iota(jnp.int32, (SUB, species), 0)
                == lax.broadcasted_iota(jnp.int32, (SUB, species), 1))
    pw_col = jnp.sum(jnp.where(diagonal, prior[...], 0.0), axis=1, keepdims=True)
    pw[...] = jnp.broadcast_to(pw_col, (SUB, LEV))

    def build(slot, g):
        first = source[slot, g, species:species + 1, :].astype(jnp.int32)
        mine = [u for u in range(span) if group_of[u] == g]
        cell = None
        for u in mine:
            own = tab[slot, 0:tile, u * rays:(u + 1) * rays]
            length = tab[slot, tile:2 * tile, u * rays:(u + 1) * rays]
            here = (first <= u) & (first + reach >= u)
            if cell is None:
                cell, total, there = own, length, here
            else:
                cell = jnp.where(here, own, cell)
                total = jnp.where(here, length, total)
                there = there | here
        cell = cell.astype(jnp.int32)
        band = lax.rem(lax.div(cell[0:1, :], LEV), CLAT)
        at = pl.ds(g * rays, rays)
        latkey[slot, :, at] = jnp.broadcast_to(jnp.where(there, band, -1), (SUB, rays))
        key = lax.div(cell, CLAT * LEV) * LEV + lax.rem(cell, LEV)
        hi = total.astype(bf16).astype(f32)
        lo = total - hi
        shape = (HALF // 16, 16, rays)
        rows = lax.broadcasted_iota(jnp.int32, shape, 0) * 16 + lax.broadcasted_iota(jnp.int32, shape, 1)
        rows = rows.astype(f32).astype(bf16)
        for half in range(CLON * LEV // HALF):
            acc_hi = jnp.zeros(shape, bf16)
            acc_lo = jnp.zeros(shape, bf16)
            near = (key - half * HALF).astype(f32)
            for m in range(tile):
                wide = lambda v: jnp.broadcast_to(v[m:m + 1, :], (16, rays)).astype(bf16)[None]
                hit = rows == wide(near)
                acc_hi = jnp.where(hit, wide(hi), acc_hi)
                acc_lo = jnp.where(hit, wide(lo), acc_lo)
            w_hi[slot, half * HALF:(half + 1) * HALF, at] = acc_hi.reshape(HALF, rays)
            w_lo[slot, half * HALF:(half + 1) * HALF, at] = acc_lo.reshape(HALF, rays)

    def await_source(o, g):
        if (o, g) != (0, 0):
            source_copies[(o, g)].wait()

    for o in range(n_orbit):
        if o > 0:
            tab_copies[o - 1].wait()
        for g in range(len(groups)):
            await_source(o, g)
            build(lax.rem(orbit + n_orbit - o, n_orbit), g)

    def back(images):
        total = None
        for o in range(n_orbit):
            part = back_orbit(o, images[o])
            total = part if total is None else total + part
        return total

    def back_orbit(o, per_group):
        y = jnp.concatenate(per_group, axis=1)
        y_hi = y.astype(bf16).astype(f32)
        y_lo = y - y_hi
        band = latkey[o]
        high = jnp.concatenate([jnp.where(band == b, y_hi, 0.0) for b in range(CLAT)], axis=0)
        low = jnp.concatenate([jnp.where(band == b, y_lo, 0.0) for b in range(CLAT)], axis=0)
        high = high.astype(bf16)
        both = jnp.concatenate([high, low.astype(bf16)], axis=0)
        first = lax.dot_general(both, w_hi[o], NT_DIMS, preferred_element_type=f32)
        second = lax.dot_general(high, w_lo[o], NT_DIMS, preferred_element_type=f32)
        rows = CLAT * SUB
        return first[0:rows] + (first[rows:] + second)

    def product(turn, send_sums=None, between=None):
        v_ref = ops.at[turn]
        last = (CLON - 1) * LEV
        halos = [
            pltpu.make_async_remote_copy(
                src_ref=src, dst_ref=dst, send_sem=halo_ssem.at[turn, side],
                recv_sem=halo_rsem.at[turn, side], device_id=device, device_id_type=MESH)
            for side, (src, dst, device) in enumerate((
                (v_ref.at[(CLAT - 1) * SUB:CLAT * SUB, :], lat_halo.at[turn, 0],
                 (orbit, lon, lax.rem(lat + 1, n_lat))),
                (v_ref.at[0:SUB, :], lat_halo.at[turn, 1], (orbit, lon, lax.rem(lat + n_lat - 1, n_lat))),
                (v_ref.at[:, last:last + LEV], lon_halo.at[turn, 0],
                 (orbit, lax.rem(lon + 1, n_lon), lat)),
                (v_ref.at[:, 0:LEV], lon_halo.at[turn, 1],
                 (orbit, lax.rem(lon + n_lon - 1, n_lon), lat)),
            ))
        ]
        for copy in halos[:2]:
            copy.start()
        v = v_ref[...]
        rows = CLAT * SUB
        v_high = v.astype(bf16)
        t_copies = [[] for _ in range(n_orbit)]
        v_both = jnp.concatenate([v_high, (v - v_high.astype(f32)).astype(bf16)], axis=0)
        for o in range(n_orbit):
            first = jnp.dot(v_both, w_hi[o], preferred_element_type=f32)
            second = jnp.dot(v_high, w_lo[o], preferred_element_type=f32)
            sums = first[0:rows] + (first[rows:] + second)
            band = latkey[o]
            picked = jnp.zeros((SUB, len(groups) * rays), f32)
            for b in range(CLAT):
                picked = jnp.where(band == b, sums[b * SUB:(b + 1) * SUB], picked)
            for g in range(len(groups)):
                t_send[turn, o, g] = picked[:, g * rays:(g + 1) * rays]
            for k, distance in enumerate(peers):
                if k == 0:
                    continue
                copy = pltpu.make_async_remote_copy(
                    src_ref=t_send.at[turn, o], dst_ref=t_recv.at[turn, k - 1, o],
                    send_sem=t_ssem.at[turn, k, o], recv_sem=t_rsem.at[turn, k, o],
                    device_id=(orbit, lax.rem(lon + distance, n_lon), lat), device_id_type=MESH)
                copy.start()
                t_copies[o].append(copy)
            if o == 0 and send_sums is not None:
                send_sums()

        for copy in halos[2:]:
            copy.start()
        for copy in halos[:2]:
            copy.wait()
        lane = lax.broadcasted_iota(jnp.int32, (rows, LEV), 1)
        weight = jnp.concatenate([pw[...]] * CLAT, axis=0)
        column = lambda c: v_ref[:, c * LEV:(c + 1) * LEV]
        for c in range(CLON):
            here = column(c)
            south = jnp.where(lat == 0, 0.0, lat_halo[turn, 0, :, c * LEV:(c + 1) * LEV])
            north = jnp.where(lat == n_lat - 1, 0.0, lat_halo[turn, 1, :, c * LEV:(c + 1) * LEV])
            around = jnp.concatenate([south, here[:-SUB]], axis=0)
            around = around + jnp.concatenate([here[SUB:], north], axis=0)
            for beside in (c - 1, c + 1):
                if 0 <= beside < CLON:
                    around = around + column(beside)
            around = around + jnp.where(lane == 0, 0.0, pltpu.roll(here, 1, 1))
            around = around + jnp.where(lane == LEV - 1, 0.0, pltpu.roll(here, LEV - 1, 1))
            prior_acc[:, c * LEV:(c + 1) * LEV] = weight * (6.0 * here - around)

        if between is not None:
            between()
        result = prior_acc[...]
        for o in range(n_orbit):
            for copy in t_copies[o]:
                copy.wait()
            per_group = []
            for g, d in enumerate(groups):
                total = t_send[turn, o, g]
                for k, distance in enumerate(peers):
                    theirs = (d - distance) % n_lon
                    if k > 0 and theirs in groups:
                        total = total + t_recv[turn, k - 1, o, groups.index(theirs)]
                image = jnp.zeros((SUB, rays), f32)
                for t in range(species):
                    image = image + gcol[t] * total[t:t + 1, :]
                per_group.append(image)
            result = result + back_orbit(o, per_group)
        for copy in halos[2:]:
            copy.wait()
        west = result[:, :LEV] - weight * lon_halo[turn, 0]
        east = result[:, last:] - weight * lon_halo[turn, 1]
        return jnp.concatenate([west, result[:, LEV:last], east], axis=1)

    def inner(a, b):
        whole = a * b
        lanes = sum(whole[:, c * LEV:(c + 1) * LEV] for c in range(CLON))
        return jnp.sum(jnp.sum(lanes, axis=0, keepdims=True), axis=1, keepdims=True)

    def form_dots(turn):
        r = vec_r[...]
        w = ops[turn + 1] if turn + 1 < ITERS else vec_w[...]
        terms = [inner(r, r), inner(r, w)]
        if turn > 0:
            terms += [inner(r, vec_s[...]), inner(vec_d[...], w)]
        spot = lax.broadcasted_iota(jnp.int32, (1, LEV), 1)
        row = jnp.zeros((1, LEV), f32)
        for i, term in enumerate(terms):
            row = jnp.where(spot == i, term, row)
        d_recv[turn, 0] = row

    def send_dots(turn):
        def send(k):
            pltpu.make_async_remote_copy(
                src_ref=d_recv.at[turn, 0], dst_ref=d_recv.at[turn, k + 1],
                send_sem=d_ssem.at[turn], recv_sem=d_rsem.at[turn],
                device_id=plane_peer(k + 1), device_id_type=MESH).start()

        each(planes - 1, send)

    def finish_dots(turn):
        pltpu.make_async_remote_copy(
            src_ref=d_recv.at[turn, pl.ds(1, planes - 1)], dst_ref=d_recv.at[turn, pl.ds(1, planes - 1)],
            send_sem=d_ssem.at[turn], recv_sem=d_rsem.at[turn],
            device_id=plane_peer(1), device_id_type=MESH).wait()
        total = jnp.zeros((1, LEV), f32)
        for f in range(planes):
            total = total + d_recv[turn, lax.rem(place + planes - f, planes)]
        return [total[:, i:i + 1] for i in range(4)]

    images = [[jnp.where(sublane < species, source[o, g], 0.0) for g in range(len(groups))]
              for o in range(n_orbit)]
    right_side = back(images)
    vec_r[...] = right_side
    ops[0] = right_side
    ops[1] = product(0)
    kept = {}

    def advance(turn):
        norm, cross, cross_s, cross_d = finish_dots(turn)
        w = ops[turn + 1] if turn + 1 < ITERS else vec_w[...]
        if turn == 0:
            kept["curvature"] = cross
            alpha = norm / cross
            direction = vec_r[...]
            moved = w
            vec_x[...] = alpha * direction
        else:
            beta = norm / kept["norm"]
            kept["beta"] = beta
            kept["curvature"] = cross + beta * (cross_s + cross_d) + beta * beta * kept["curvature"]
            alpha = norm / kept["curvature"]
            direction = vec_r[...] + beta * vec_d[...]
            moved = w + beta * vec_s[...]
            vec_x[...] = vec_x[...] + alpha * direction
        vec_r[...] = vec_r[...] - alpha * moved
        if turn < ITERS - 1:
            vec_d[...] = direction
            vec_s[...] = moved
        kept["norm"] = norm
        kept["alpha"] = alpha

    for turn in range(ITERS - 1):
        form_dots(turn)
        image = product(turn + 1, lambda: send_dots(turn), lambda: advance(turn))
        twice = image if turn == 0 else image + kept["beta"] * vec_z[...]
        vec_z[...] = twice
        moved_on = ops[turn + 1] - kept["alpha"] * twice
        if turn + 2 < ITERS:
            ops[turn + 2] = moved_on
        else:
            vec_w[...] = moved_on
    form_dots(ITERS - 1)
    send_dots(ITERS - 1)
    advance(ITERS - 1)
    x_out[...] = vec_x[...]
    r_out[...] = vec_r[...]


def body(sizes, observed, ray_start, tile_cells, tile_lengths, channel_kernel, noise_weight, prior_weight):
    n_orbit, n_lon, n_lat = sizes
    species, channels = channel_kernel.shape
    rays = ray_start.shape[0]
    rows, tile = tile_cells.shape
    groups = len(residues(NT - 1, n_lon))
    peers = len(residues(2 * (NT - 1), n_lon))
    flat = (CLAT * SUB, CLON * LEV)
    vmem = pltpu.VMEM
    dma = pltpu.SemaphoreType.DMA
    out = jax.ShapeDtypeStruct(flat, f32)
    solved, left = pl.pallas_call(
        functools.partial(kernel, sizes),
        out_shape=(out, out),
        in_specs=[pl.BlockSpec(memory_space=pltpu.HBM)] * 7,
        out_specs=[pl.BlockSpec(memory_space=pltpu.VMEM)] * 2,
        scratch_shapes=[
            vmem((channels, rays), f32),
            vmem((1, rays), jnp.int32),
            vmem((tile, rows), jnp.int32),
            vmem((tile, rows), f32),
            vmem((species, channels), f32),
            vmem((1, channels), f32),
            vmem((1, species), f32),
            dma((7,)),
            vmem((SUB, channels), f32),
            vmem((species, SUB, LEV), f32),
            vmem((SUB, LEV), f32),
            vmem((n_orbit, 2 * tile, rows), f32),
            vmem((n_orbit, CLON * LEV, groups * rays), bf16),
            vmem((n_orbit, CLON * LEV, groups * rays), bf16),
            vmem((n_orbit, SUB, groups * rays), jnp.int32),
            vmem((n_orbit, groups, SUB, rays), f32),
            vmem((ITERS,) + flat, f32),
            vmem((ITERS, 2, flat[0], LEV), f32),
            vmem((ITERS, 2, SUB, flat[1]), f32),
            vmem((ITERS, n_orbit, groups, SUB, rays), f32),
            vmem((ITERS, peers - 1, n_orbit, groups, SUB, rays), f32),
            vmem((ITERS, n_lon * n_lat, 1, LEV), f32),
        ] + [vmem(flat, f32)] * 7 + [
            dma((n_orbit, groups)), dma((n_orbit, groups)),
            dma((n_orbit,)), dma((n_orbit,)),
            dma((ITERS, 4)), dma((ITERS, 4)),
            dma((ITERS, peers, n_orbit)), dma((ITERS, peers, n_orbit)),
            dma((ITERS,)), dma((ITERS,)),
        ],
        compiler_params=pltpu.CompilerParams(
            collective_id=0, has_side_effects=True, vmem_limit_bytes=VMEM_BYTES),
    )(
        observed.T, ray_start.reshape(1, rays), tile_cells.T, tile_lengths.T,
        channel_kernel, noise_weight.reshape(1, channels), prior_weight.reshape(1, species),
    )

    def placed(field):
        shaped = field.reshape(CLAT, SUB, CLON, LEV)[:, :species]
        return shaped.transpose(1, 2, 0, 3)

    return placed(solved), placed(left)


def solution(mesh):
    sizes = tuple(mesh.shape[name] for name in ("orbit", "lon", "lat"))
    return jax.shard_map(
        functools.partial(body, sizes),
        mesh=mesh,
        in_specs=(
            P(("orbit", "lon", "lat"), None),
            P(("orbit", "lon", "lat")),
            P(("orbit", "lon", "lat"), None),
            P(("orbit", "lon", "lat"), None),
            P(),
            P(),
            P(),
        ),
        out_specs=(P(None, "lon", "lat", None), P(None, "lon", "lat", None)),
        check_vma=False,
    )
```

```python
import functools

import jax
import jax.numpy as jnp
from jax import lax
from jax.experimental import pallas as pl
from jax.experimental.pallas import tpu as pltpu
from jax.sharding import PartitionSpec as P

CLON = 4
CLAT = 8
LEV = 128
NT = 3
ITERS = 4
SUB = 8
HALF = 256
VMEM_BYTES = 60 * 1024 * 1024

highest = lax.Precision.HIGHEST
MESH = pl.DeviceIdType.MESH
f32 = jnp.float32
bf16 = jnp.bfloat16
NT_DIMS = (((1,), (1,)), ((), ()))


def residues(reach, size):
    found = []
    for d in range(-reach, reach + 1):
        if d % size not in found:
            found.append(d % size)
    found.remove(0)
    return [0] + found


def kernel(sizes, observed_in, starts_in, cells_in, lengths_in, channel_in, noise_in, prior_in,
           x_out, r_out, observed, starts, cells, lengths, channel, noise, prior, load_sem,
           ck8, gcol, pw, tab, w_hi, w_lo, latkey, source, ops, lon_halo, lat_halo,
           t_send, t_recv, lon_sums, lat_sums, prior_acc, vec_x, vec_r, vec_w, vec_d, vec_s, vec_z,
           source_ssem, source_rsem, tab_ssem, tab_rsem, halo_ssem, halo_rsem,
           t_ssem, t_rsem, d_ssem, d_rsem):
    n_orbit, n_lon, n_lat = sizes
    reach = NT - 1
    span = 2 * NT - 1
    species, channels = channel.shape
    rays = starts.shape[1]
    tile = cells.shape[0]
    groups = residues(reach, n_lon)
    peers = residues(2 * reach, n_lon)
    group_of = [groups.index((u - reach) % n_lon) for u in range(span)]
    orbit = lax.axis_index("orbit")
    lon = lax.axis_index("lon")
    lat = lax.axis_index("lat")

    barrier = pltpu.get_barrier_semaphore()
    loads = [
        pltpu.make_async_copy(src, dst, load_sem.at[i])
        for i, (src, dst) in enumerate((
            (cells_in, cells), (lengths_in, lengths), (observed_in, observed), (channel_in, channel),
            (noise_in, noise), (starts_in, starts), (prior_in, prior)))
    ]
    for load in loads:
        load.start()

    def lon_peer(k):
        return (orbit, lax.rem(lon + k, n_lon), lat)

    def lat_peer(k):
        return (orbit, lon, lax.rem(lat + k, n_lat))

    for peer, count in ((lat_peer, n_lat), (lon_peer, n_lon)):
        for k in range(1, count):
            pl.semaphore_signal(barrier, inc=1, device_id=peer(k), device_id_type=MESH)
    for o in range(1, n_orbit):
        for d in groups:
            pl.semaphore_signal(
                barrier, inc=1, device_id_type=MESH,
                device_id=(lax.rem(orbit + o, n_orbit), lax.rem(lon + d, n_lon), lat))

    for load in loads[:2]:
        load.wait()
    own_cells = cells[...]
    own_lengths = lengths[...]
    totals = jnp.zeros_like(own_lengths)
    for m in range(tile):
        totals = totals + jnp.where(own_cells == own_cells[m:m + 1, :], own_lengths[m:m + 1, :], 0.0)
    tab[orbit, 0:tile, :] = own_cells.astype(f32)
    tab[orbit, tile:2 * tile, :] = totals

    pl.semaphore_wait(barrier, n_lat + n_lon - 2 + (n_orbit - 1) * len(groups))
    sent = []

    tab_copies = []
    for o in range(1, n_orbit):
        copy = pltpu.make_async_remote_copy(
            src_ref=tab.at[orbit], dst_ref=tab.at[orbit],
            send_sem=tab_ssem.at[o], recv_sem=tab_rsem.at[o],
            device_id=(lax.rem(orbit + o, n_orbit), lon, lat), device_id_type=MESH)
        copy.start()
        tab_copies.append(copy)
        sent.append(copy)
    for load in loads[2:]:
        load.wait()
    ck8[...] = jnp.zeros_like(ck8)
    ck8[0:species, :] = channel[...]
    kernel_rows = ck8[...]
    weighted = kernel_rows * noise[...]
    sublane = lax.broadcasted_iota(jnp.int32, (SUB, LEV), 0)
    own_source = jnp.dot(weighted, observed[...], precision=highest, preferred_element_type=f32)
    source[orbit, 0] = jnp.where(sublane == species, starts[...].astype(f32), own_source)
    source_copies = {}
    for o in range(n_orbit):
        for g, d in enumerate(groups):
            if o == 0 and g == 0:
                continue
            copy = pltpu.make_async_remote_copy(
                src_ref=source.at[orbit, 0], dst_ref=source.at[orbit, g],
                send_sem=source_ssem.at[o, g], recv_sem=source_rsem.at[o, g],
                device_id=(lax.rem(orbit + o, n_orbit), lax.rem(lon + d, n_lon), lat),
                device_id_type=MESH)
            copy.start()
            source_copies[(o, g)] = copy
            sent.append(copy)

    gram = lax.dot_general(weighted, kernel_rows, NT_DIMS, precision=highest,
                           preferred_element_type=f32)
    for t in range(species):
        gcol[t] = jnp.broadcast_to(gram[:, t:t + 1], (SUB, LEV))
    diagonal = (lax.broadcasted_iota(jnp.int32, (SUB, species), 0)
                == lax.broadcasted_iota(jnp.int32, (SUB, species), 1))
    pw_col = jnp.sum(jnp.where(diagonal, prior[...], 0.0), axis=1, keepdims=True)
    pw[...] = jnp.broadcast_to(pw_col, (SUB, LEV))

    def build(slot, g):
        first = source[slot, g, species:species + 1, :].astype(jnp.int32)
        mine = [u for u in range(span) if group_of[u] == g]
        cell = None
        for u in mine:
            own = tab[slot, 0:tile, u * rays:(u + 1) * rays]
            length = tab[slot, tile:2 * tile, u * rays:(u + 1) * rays]
            here = (first <= u) & (first + reach >= u)
            if cell is None:
                cell, total, there = own, length, here
            else:
                cell = jnp.where(here, own, cell)
                total = jnp.where(here, length, total)
                there = there | here
        cell = cell.astype(jnp.int32)
        band = lax.rem(lax.div(cell[0:1, :], LEV), CLAT)
        at = pl.ds(g * rays, rays)
        latkey[slot, :, at] = jnp.broadcast_to(jnp.where(there, band, -1), (SUB, rays))
        key = lax.div(cell, CLAT * LEV) * LEV + lax.rem(cell, LEV)
        hi = total.astype(bf16).astype(f32)
        lo = total - hi
        shape = (HALF // 16, 16, rays)
        rows = lax.broadcasted_iota(jnp.int32, shape, 0) * 16 + lax.broadcasted_iota(jnp.int32, shape, 1)
        rows = rows.astype(f32).astype(bf16)
        for half in range(CLON * LEV // HALF):
            acc_hi = jnp.zeros(shape, bf16)
            acc_lo = jnp.zeros(shape, bf16)
            near = (key - half * HALF).astype(f32)
            for m in range(tile):
                wide = lambda v: jnp.broadcast_to(v[m:m + 1, :], (16, rays)).astype(bf16)[None]
                hit = rows == wide(near)
                acc_hi = jnp.where(hit, wide(hi), acc_hi)
                acc_lo = jnp.where(hit, wide(lo), acc_lo)
            w_hi[slot, half * HALF:(half + 1) * HALF, at] = acc_hi.reshape(HALF, rays)
            w_lo[slot, half * HALF:(half + 1) * HALF, at] = acc_lo.reshape(HALF, rays)

    def await_source(o, g):
        if (o, g) != (0, 0):
            source_copies[(o, g)].wait_recv()

    for o in range(n_orbit):
        if o > 0:
            tab_copies[o - 1].wait_recv()
        for g in range(len(groups)):
            await_source(o, g)
            build(lax.rem(orbit + n_orbit - o, n_orbit), g)

    def back(images):
        total = None
        for o in range(n_orbit):
            part = back_orbit(o, images[o])
            total = part if total is None else total + part
        return total

    def back_orbit(o, per_group):
        y = jnp.concatenate(per_group, axis=1)
        y_hi = y.astype(bf16).astype(f32)
        y_lo = y - y_hi
        band = latkey[o]
        high = jnp.concatenate([jnp.where(band == b, y_hi, 0.0) for b in range(CLAT)], axis=0)
        low = jnp.concatenate([jnp.where(band == b, y_lo, 0.0) for b in range(CLAT)], axis=0)
        high = high.astype(bf16)
        both = jnp.concatenate([high, low.astype(bf16)], axis=0)
        first = lax.dot_general(both, w_hi[o], NT_DIMS, preferred_element_type=f32)
        second = lax.dot_general(high, w_lo[o], NT_DIMS, preferred_element_type=f32)
        rows = CLAT * SUB
        return first[0:rows] + (first[rows:] + second)

    def product(turn, pass_sums=None):
        v_ref = ops.at[turn]
        last = (CLON - 1) * LEV
        halos = [
            pltpu.make_async_remote_copy(
                src_ref=src, dst_ref=dst, send_sem=halo_ssem.at[turn, side],
                recv_sem=halo_rsem.at[turn, side], device_id=device, device_id_type=MESH)
            for side, (src, dst, device) in enumerate((
                (v_ref.at[(CLAT - 1) * SUB:CLAT * SUB, :], lat_halo.at[turn, 0],
                 (orbit, lon, lax.rem(lat + 1, n_lat))),
                (v_ref.at[0:SUB, :], lat_halo.at[turn, 1], (orbit, lon, lax.rem(lat + n_lat - 1, n_lat))),
                (v_ref.at[:, last:last + LEV], lon_halo.at[turn, 0],
                 (orbit, lax.rem(lon + 1, n_lon), lat)),
                (v_ref.at[:, 0:LEV], lon_halo.at[turn, 1],
                 (orbit, lax.rem(lon + n_lon - 1, n_lon), lat)),
            ))
        ]
        sent.extend(halos)
        for copy in halos[:2]:
            copy.start()
        v = v_ref[...]
        rows = CLAT * SUB
        v_high = v.astype(bf16)
        t_copies = [[] for _ in range(n_orbit)]
        v_both = jnp.concatenate([v_high, (v - v_high.astype(f32)).astype(bf16)], axis=0)
        for o in range(n_orbit):
            first = jnp.dot(v_both, w_hi[o], preferred_element_type=f32)
            second = jnp.dot(v_high, w_lo[o], preferred_element_type=f32)
            sums = first[0:rows] + (first[rows:] + second)
            band = latkey[o]
            picked = jnp.zeros((SUB, len(groups) * rays), f32)
            for b in range(CLAT):
                picked = jnp.where(band == b, sums[b * SUB:(b + 1) * SUB], picked)
            for g in range(len(groups)):
                t_send[turn, o, g] = picked[:, g * rays:(g + 1) * rays]
            for k, distance in enumerate(peers):
                if k == 0:
                    continue
                copy = pltpu.make_async_remote_copy(
                    src_ref=t_send.at[turn, o], dst_ref=t_recv.at[turn, k - 1, o],
                    send_sem=t_ssem.at[turn, k, o], recv_sem=t_rsem.at[turn, k, o],
                    device_id=(orbit, lax.rem(lon + distance, n_lon), lat), device_id_type=MESH)
                copy.start()
                t_copies[o].append(copy)
                sent.append(copy)
        for copy in halos[2:]:
            copy.start()
        if pass_sums is not None:
            pass_sums()
        for copy in halos[:2]:
            copy.wait_recv()
        lane = lax.broadcasted_iota(jnp.int32, (rows, LEV), 1)
        weight = jnp.concatenate([pw[...]] * CLAT, axis=0)
        column = lambda c: v_ref[:, c * LEV:(c + 1) * LEV]
        for c in range(CLON):
            here = column(c)
            south = jnp.where(lat == 0, 0.0, lat_halo[turn, 0, :, c * LEV:(c + 1) * LEV])
            north = jnp.where(lat == n_lat - 1, 0.0, lat_halo[turn, 1, :, c * LEV:(c + 1) * LEV])
            around = jnp.concatenate([south, here[:-SUB]], axis=0)
            around = around + jnp.concatenate([here[SUB:], north], axis=0)
            for beside in (c - 1, c + 1):
                if 0 <= beside < CLON:
                    around = around + column(beside)
            around = around + jnp.where(lane == 0, 0.0, pltpu.roll(here, 1, 1))
            around = around + jnp.where(lane == LEV - 1, 0.0, pltpu.roll(here, LEV - 1, 1))
            prior_acc[:, c * LEV:(c + 1) * LEV] = weight * (6.0 * here - around)

        result = prior_acc[...]
        for o in range(n_orbit):
            for copy in t_copies[o]:
                copy.wait_recv()
            per_group = []
            for g, d in enumerate(groups):
                total = t_send[turn, o, g]
                for k, distance in enumerate(peers):
                    theirs = (d - distance) % n_lon
                    if k > 0 and theirs in groups:
                        total = total + t_recv[turn, k - 1, o, groups.index(theirs)]
                image = jnp.zeros((SUB, rays), f32)
                for t in range(species):
                    image = image + gcol[t] * total[t:t + 1, :]
                per_group.append(image)
            result = result + back_orbit(o, per_group)
        for copy in halos[2:]:
            copy.wait_recv()
        west = result[:, :LEV] - weight * lon_halo[turn, 0]
        east = result[:, last:] - weight * lon_halo[turn, 1]
        return jnp.concatenate([west, result[:, LEV:last], east], axis=1)

    def inner(a, b):
        whole = a * b
        lanes = sum(whole[:, c * LEV:(c + 1) * LEV] for c in range(CLON))
        return jnp.sum(jnp.sum(lanes, axis=0, keepdims=True), axis=1, keepdims=True)

    def form_dots(turn):
        r = vec_r[...]
        w = ops[turn + 1] if turn + 1 < ITERS else vec_w[...]
        terms = [inner(r, r), inner(r, w)]
        if turn > 0:
            terms += [inner(r, vec_s[...]), inner(vec_d[...], w)]
        spot = lax.broadcasted_iota(jnp.int32, (1, LEV), 1)
        row = jnp.zeros((1, LEV), f32)
        for i, term in enumerate(terms):
            row = jnp.where(spot == i, term, row)
        share(turn, row, lon_sums, lon_peer, n_lon, 0)

    def share(turn, row, sums, peer, count, stage):
        sums[turn, 0] = row
        for k in range(1, count):
            pltpu.make_async_remote_copy(
                src_ref=sums.at[turn, 0], dst_ref=sums.at[turn, k],
                send_sem=d_ssem.at[turn, stage], recv_sem=d_rsem.at[turn, stage],
                device_id=peer(k), device_id_type=MESH).start()

    def gather(turn, sums, peer, count, stage, index):
        whole = pltpu.make_async_remote_copy(
            src_ref=sums.at[turn, pl.ds(1, count - 1)], dst_ref=sums.at[turn, pl.ds(1, count - 1)],
            send_sem=d_ssem.at[turn, stage], recv_sem=d_rsem.at[turn, stage],
            device_id=peer(1), device_id_type=MESH)
        whole.wait_recv()
        sent.append(whole)
        total = jnp.zeros((1, LEV), f32)
        for f in range(count):
            total = total + sums[turn, lax.rem(index + count - f, count)]
        return total

    def pass_dots(turn):
        row = gather(turn, lon_sums, lon_peer, n_lon, 0, lon)
        share(turn, row, lat_sums, lat_peer, n_lat, 1)

    def finish_dots(turn):
        total = gather(turn, lat_sums, lat_peer, n_lat, 1, lat)
        return [total[:, i:i + 1] for i in range(4)]

    images = [[jnp.where(sublane < species, source[o, g], 0.0) for g in range(len(groups))]
              for o in range(n_orbit)]
    right_side = back(images)
    vec_r[...] = right_side
    ops[0] = right_side
    ops[1] = product(0)
    kept = {}

    def advance(turn):
        norm, cross, cross_s, cross_d = finish_dots(turn)
        w = ops[turn + 1] if turn + 1 < ITERS else vec_w[...]
        if turn == 0:
            kept["curvature"] = cross
            alpha = norm / cross
            direction = vec_r[...]
            moved = w
            vec_x[...] = alpha * direction
        else:
            beta = norm / kept["norm"]
            kept["beta"] = beta
            kept["curvature"] = cross + beta * (cross_s + cross_d) + beta * beta * kept["curvature"]
            alpha = norm / kept["curvature"]
            direction = vec_r[...] + beta * vec_d[...]
            moved = w + beta * vec_s[...]
            vec_x[...] = vec_x[...] + alpha * direction
        vec_r[...] = vec_r[...] - alpha * moved
        if turn < ITERS - 1:
            vec_d[...] = direction
            vec_s[...] = moved
        kept["norm"] = norm
        kept["alpha"] = alpha

    for turn in range(ITERS - 1):
        form_dots(turn)
        image = product(turn + 1, lambda: pass_dots(turn))
        advance(turn)
        twice = image if turn == 0 else image + kept["beta"] * vec_z[...]
        vec_z[...] = twice
        moved_on = ops[turn + 1] - kept["alpha"] * twice
        if turn + 2 < ITERS:
            ops[turn + 2] = moved_on
        else:
            vec_w[...] = moved_on
    form_dots(ITERS - 1)
    pass_dots(ITERS - 1)
    advance(ITERS - 1)
    x_out[...] = vec_x[...]
    r_out[...] = vec_r[...]
    for copy in sent:
        copy.wait_send()


def body(sizes, observed, ray_start, tile_cells, tile_lengths, channel_kernel, noise_weight, prior_weight):
    n_orbit, n_lon, n_lat = sizes
    species, channels = channel_kernel.shape
    rays = ray_start.shape[0]
    rows, tile = tile_cells.shape
    groups = len(residues(NT - 1, n_lon))
    peers = len(residues(2 * (NT - 1), n_lon))
    flat = (CLAT * SUB, CLON * LEV)
    vmem = pltpu.VMEM
    dma = pltpu.SemaphoreType.DMA
    out = jax.ShapeDtypeStruct(flat, f32)
    solved, left = pl.pallas_call(
        functools.partial(kernel, sizes),
        out_shape=(out, out),
        in_specs=[pl.BlockSpec(memory_space=pltpu.HBM)] * 7,
        out_specs=[pl.BlockSpec(memory_space=pltpu.VMEM)] * 2,
        scratch_shapes=[
            vmem((channels, rays), f32),
            vmem((1, rays), jnp.int32),
            vmem((tile, rows), jnp.int32),
            vmem((tile, rows), f32),
            vmem((species, channels), f32),
            vmem((1, channels), f32),
            vmem((1, species), f32),
            dma((7,)),
            vmem((SUB, channels), f32),
            vmem((species, SUB, LEV), f32),
            vmem((SUB, LEV), f32),
            vmem((n_orbit, 2 * tile, rows), f32),
            vmem((n_orbit, CLON * LEV, groups * rays), bf16),
            vmem((n_orbit, CLON * LEV, groups * rays), bf16),
            vmem((n_orbit, SUB, groups * rays), jnp.int32),
            vmem((n_orbit, groups, SUB, rays), f32),
            vmem((ITERS,) + flat, f32),
            vmem((ITERS, 2, flat[0], LEV), f32),
            vmem((ITERS, 2, SUB, flat[1]), f32),
            vmem((ITERS, n_orbit, groups, SUB, rays), f32),
            vmem((ITERS, peers - 1, n_orbit, groups, SUB, rays), f32),
            vmem((ITERS, n_lon, 1, LEV), f32),
            vmem((ITERS, n_lat, 1, LEV), f32),
        ] + [vmem(flat, f32)] * 7 + [
            dma((n_orbit, groups)), dma((n_orbit, groups)),
            dma((n_orbit,)), dma((n_orbit,)),
            dma((ITERS, 4)), dma((ITERS, 4)),
            dma((ITERS, peers, n_orbit)), dma((ITERS, peers, n_orbit)),
            dma((ITERS, 2)), dma((ITERS, 2)),
        ],
        compiler_params=pltpu.CompilerParams(
            collective_id=0, has_side_effects=True, vmem_limit_bytes=VMEM_BYTES),
    )(
        observed.T, ray_start.reshape(1, rays), tile_cells.T, tile_lengths.T,
        channel_kernel, noise_weight.reshape(1, channels), prior_weight.reshape(1, species),
    )

    def placed(field):
        shaped = field.reshape(CLAT, SUB, CLON, LEV)[:, :species]
        return shaped.transpose(1, 2, 0, 3)

    return placed(solved), placed(left)


def solution(mesh):
    sizes = tuple(mesh.shape[name] for name in ("orbit", "lon", "lat"))
    return jax.shard_map(
        functools.partial(body, sizes),
        mesh=mesh,
        in_specs=(
            P(("orbit", "lon", "lat"), None),
            P(("orbit", "lon", "lat")),
            P(("orbit", "lon", "lat"), None),
            P(("orbit", "lon", "lat"), None),
            P(),
            P(),
            P(),
        ),
        out_specs=(P(None, "lon", "lat", None), P(None, "lon", "lat", None)),
        check_vma=False,
    )
```

```python
import functools

import jax
import jax.numpy as jnp
from jax import lax
from jax.experimental import pallas as pl
from jax.experimental.pallas import tpu as pltpu
from jax.sharding import PartitionSpec as P

CLON = 4
CLAT = 8
LEV = 128
NT = 3
ITERS = 4
SUB = 8
HALF = 256
VMEM_BYTES = 60 * 1024 * 1024

highest = lax.Precision.HIGHEST
MESH = pl.DeviceIdType.MESH
f32 = jnp.float32
bf16 = jnp.bfloat16
NT_DIMS = (((1,), (1,)), ((), ()))


def each(count, step):
    if count <= 16:
        for k in range(count):
            step(k)
    else:
        lax.fori_loop(0, count, lambda k, c: (step(k), c)[1], 0)


def residues(reach, size):
    found = []
    for d in range(-reach, reach + 1):
        if d % size not in found:
            found.append(d % size)
    found.remove(0)
    return [0] + found


def kernel(sizes, observed_in, starts_in, cells_in, lengths_in, channel_in, noise_in, prior_in,
           x_out, r_out, observed, starts, cells, lengths, channel, noise, prior, load_sem,
           ck8, gcol, pw, tab, w_hi, w_lo, latkey, source, ops, lon_halo, lat_halo,
           t_send, t_recv, plane_sums, prior_acc, vec_x, vec_r, vec_w, vec_d, vec_s, vec_z,
           source_ssem, source_rsem, tab_ssem, tab_rsem, halo_ssem, halo_rsem,
           t_ssem, t_rsem, d_ssem, d_rsem):
    n_orbit, n_lon, n_lat = sizes
    reach = NT - 1
    span = 2 * NT - 1
    species, channels = channel.shape
    rays = starts.shape[1]
    tile = cells.shape[0]
    groups = residues(reach, n_lon)
    peers = residues(2 * reach, n_lon)
    group_of = [groups.index((u - reach) % n_lon) for u in range(span)]
    planes = n_lon * n_lat
    orbit = lax.axis_index("orbit")
    lon = lax.axis_index("lon")
    lat = lax.axis_index("lat")
    place = lon * n_lat + lat

    barrier = pltpu.get_barrier_semaphore()
    loads = [
        pltpu.make_async_copy(src, dst, load_sem.at[i])
        for i, (src, dst) in enumerate((
            (cells_in, cells), (lengths_in, lengths), (observed_in, observed), (channel_in, channel),
            (noise_in, noise), (starts_in, starts), (prior_in, prior)))
    ]
    for load in loads:
        load.start()

    def plane_peer(k):
        there = lax.rem(place + k, planes)
        return (orbit, lax.div(there, n_lat), lax.rem(there, n_lat))

    def greet(k):
        pl.semaphore_signal(barrier, inc=1, device_id=plane_peer(k + 1), device_id_type=MESH)

    each(planes - 1, greet)
    for o in range(1, n_orbit):
        for d in groups:
            pl.semaphore_signal(
                barrier, inc=1, device_id_type=MESH,
                device_id=(lax.rem(orbit + o, n_orbit), lax.rem(lon + d, n_lon), lat))

    for load in loads[:2]:
        load.wait()
    own_cells = cells[...]
    own_lengths = lengths[...]
    totals = jnp.zeros_like(own_lengths)
    for m in range(tile):
        totals = totals + jnp.where(own_cells == own_cells[m:m + 1, :], own_lengths[m:m + 1, :], 0.0)
    tab[orbit, 0:tile, :] = own_cells.astype(f32)
    tab[orbit, tile:2 * tile, :] = totals

    pl.semaphore_wait(barrier, planes - 1 + (n_orbit - 1) * len(groups))
    sent = []

    tab_copies = []
    for o in range(1, n_orbit):
        copy = pltpu.make_async_remote_copy(
            src_ref=tab.at[orbit], dst_ref=tab.at[orbit],
            send_sem=tab_ssem.at[o], recv_sem=tab_rsem.at[o],
            device_id=(lax.rem(orbit + o, n_orbit), lon, lat), device_id_type=MESH)
        copy.start()
        tab_copies.append(copy)
        sent.append(copy)
    for load in loads[2:]:
        load.wait()
    ck8[...] = jnp.zeros_like(ck8)
    ck8[0:species, :] = channel[...]
    kernel_rows = ck8[...]
    weighted = kernel_rows * noise[...]
    sublane = lax.broadcasted_iota(jnp.int32, (SUB, LEV), 0)
    own_source = jnp.dot(weighted, observed[...], precision=highest, preferred_element_type=f32)
    source[orbit, 0] = jnp.where(sublane == species, starts[...].astype(f32), own_source)
    source_copies = {}
    for o in range(n_orbit):
        for g, d in enumerate(groups):
            if o == 0 and g == 0:
                continue
            copy = pltpu.make_async_remote_copy(
                src_ref=source.at[orbit, 0], dst_ref=source.at[orbit, g],
                send_sem=source_ssem.at[o, g], recv_sem=source_rsem.at[o, g],
                device_id=(lax.rem(orbit + o, n_orbit), lax.rem(lon + d, n_lon), lat),
                device_id_type=MESH)
            copy.start()
            source_copies[(o, g)] = copy
            sent.append(copy)

    gram = lax.dot_general(weighted, kernel_rows, NT_DIMS, precision=highest,
                           preferred_element_type=f32)
    for t in range(species):
        gcol[t] = jnp.broadcast_to(gram[:, t:t + 1], (SUB, LEV))
    diagonal = (lax.broadcasted_iota(jnp.int32, (SUB, species), 0)
                == lax.broadcasted_iota(jnp.int32, (SUB, species), 1))
    pw_col = jnp.sum(jnp.where(diagonal, prior[...], 0.0), axis=1, keepdims=True)
    pw[...] = jnp.broadcast_to(pw_col, (SUB, LEV))

    def build(slot, g):
        first = source[slot, g, species:species + 1, :].astype(jnp.int32)
        mine = [u for u in range(span) if group_of[u] == g]
        cell = None
        for u in mine:
            own = tab[slot, 0:tile, u * rays:(u + 1) * rays]
            length = tab[slot, tile:2 * tile, u * rays:(u + 1) * rays]
            here = (first <= u) & (first + reach >= u)
            if cell is None:
                cell, total, there = own, length, here
            else:
                cell = jnp.where(here, own, cell)
                total = jnp.where(here, length, total)
                there = there | here
        cell = cell.astype(jnp.int32)
        band = lax.rem(lax.div(cell[0:1, :], LEV), CLAT)
        at = pl.ds(g * rays, rays)
        latkey[slot, :, at] = jnp.broadcast_to(jnp.where(there, band, -1), (SUB, rays))
        key = lax.div(cell, CLAT * LEV) * LEV + lax.rem(cell, LEV)
        hi = total.astype(bf16).astype(f32)
        lo = total - hi
        shape = (HALF // 16, 16, rays)
        rows = lax.broadcasted_iota(jnp.int32, shape, 0) * 16 + lax.broadcasted_iota(jnp.int32, shape, 1)
        rows = rows.astype(f32).astype(bf16)
        for half in range(CLON * LEV // HALF):
            acc_hi = jnp.zeros(shape, bf16)
            acc_lo = jnp.zeros(shape, bf16)
            near = (key - half * HALF).astype(f32)
            for m in range(tile):
                wide = lambda v: jnp.broadcast_to(v[m:m + 1, :], (16, rays)).astype(bf16)[None]
                hit = rows == wide(near)
                acc_hi = jnp.where(hit, wide(hi), acc_hi)
                acc_lo = jnp.where(hit, wide(lo), acc_lo)
            w_hi[slot, half * HALF:(half + 1) * HALF, at] = acc_hi.reshape(HALF, rays)
            w_lo[slot, half * HALF:(half + 1) * HALF, at] = acc_lo.reshape(HALF, rays)

    def await_source(o, g):
        if (o, g) != (0, 0):
            source_copies[(o, g)].wait_recv()

    for o in range(n_orbit):
        if o > 0:
            tab_copies[o - 1].wait_recv()
        for g in range(len(groups)):
            await_source(o, g)
            build(lax.rem(orbit + n_orbit - o, n_orbit), g)

    def back(images):
        total = None
        for o in range(n_orbit):
            part = back_orbit(o, images[o])
            total = part if total is None else total + part
        return total

    def back_orbit(o, per_group):
        y = jnp.concatenate(per_group, axis=1)
        y_hi = y.astype(bf16).astype(f32)
        y_lo = y - y_hi
        band = latkey[o]
        high = jnp.concatenate([jnp.where(band == b, y_hi, 0.0) for b in range(CLAT)], axis=0)
        low = jnp.concatenate([jnp.where(band == b, y_lo, 0.0) for b in range(CLAT)], axis=0)
        high = high.astype(bf16)
        both = jnp.concatenate([high, low.astype(bf16)], axis=0)
        first = lax.dot_general(both, w_hi[o], NT_DIMS, preferred_element_type=f32)
        second = lax.dot_general(high, w_lo[o], NT_DIMS, preferred_element_type=f32)
        rows = CLAT * SUB
        return first[0:rows] + (first[rows:] + second)

    def product(turn, pass_sums=None):
        v_ref = ops.at[turn]
        last = (CLON - 1) * LEV
        halos = [
            pltpu.make_async_remote_copy(
                src_ref=src, dst_ref=dst, send_sem=halo_ssem.at[turn, side],
                recv_sem=halo_rsem.at[turn, side], device_id=device, device_id_type=MESH)
            for side, (src, dst, device) in enumerate((
                (v_ref.at[(CLAT - 1) * SUB:CLAT * SUB, :], lat_halo.at[turn, 0],
                 (orbit, lon, lax.rem(lat + 1, n_lat))),
                (v_ref.at[0:SUB, :], lat_halo.at[turn, 1], (orbit, lon, lax.rem(lat + n_lat - 1, n_lat))),
                (v_ref.at[:, last:last + LEV], lon_halo.at[turn, 0],
                 (orbit, lax.rem(lon + 1, n_lon), lat)),
                (v_ref.at[:, 0:LEV], lon_halo.at[turn, 1],
                 (orbit, lax.rem(lon + n_lon - 1, n_lon), lat)),
            ))
        ]
        sent.extend(halos)
        for copy in halos[:2]:
            copy.start()
        v = v_ref[...]
        rows = CLAT * SUB
        v_high = v.astype(bf16)
        t_copies = [[] for _ in range(n_orbit)]
        v_both = jnp.concatenate([v_high, (v - v_high.astype(f32)).astype(bf16)], axis=0)
        for o in range(n_orbit):
            first = jnp.dot(v_both, w_hi[o], preferred_element_type=f32)
            second = jnp.dot(v_high, w_lo[o], preferred_element_type=f32)
            sums = first[0:rows] + (first[rows:] + second)
            band = latkey[o]
            picked = jnp.zeros((SUB, len(groups) * rays), f32)
            for b in range(CLAT):
                picked = jnp.where(band == b, sums[b * SUB:(b + 1) * SUB], picked)
            for g in range(len(groups)):
                t_send[turn, o, g] = picked[:, g * rays:(g + 1) * rays]
            for k, distance in enumerate(peers):
                if k == 0:
                    continue
                copy = pltpu.make_async_remote_copy(
                    src_ref=t_send.at[turn, o], dst_ref=t_recv.at[turn, k - 1, o],
                    send_sem=t_ssem.at[turn, k, o], recv_sem=t_rsem.at[turn, k, o],
                    device_id=(orbit, lax.rem(lon + distance, n_lon), lat), device_id_type=MESH)
                copy.start()
                t_copies[o].append(copy)
                sent.append(copy)
            if o == 0 and pass_sums is not None:
                pass_sums()

        for copy in halos[2:]:
            copy.start()
        for copy in halos[:2]:
            copy.wait_recv()
        lane = lax.broadcasted_iota(jnp.int32, (rows, LEV), 1)
        weight = jnp.concatenate([pw[...]] * CLAT, axis=0)
        column = lambda c: v_ref[:, c * LEV:(c + 1) * LEV]
        for c in range(CLON):
            here = column(c)
            south = jnp.where(lat == 0, 0.0, lat_halo[turn, 0, :, c * LEV:(c + 1) * LEV])
            north = jnp.where(lat == n_lat - 1, 0.0, lat_halo[turn, 1, :, c * LEV:(c + 1) * LEV])
            around = jnp.concatenate([south, here[:-SUB]], axis=0)
            around = around + jnp.concatenate([here[SUB:], north], axis=0)
            for beside in (c - 1, c + 1):
                if 0 <= beside < CLON:
                    around = around + column(beside)
            around = around + jnp.where(lane == 0, 0.0, pltpu.roll(here, 1, 1))
            around = around + jnp.where(lane == LEV - 1, 0.0, pltpu.roll(here, LEV - 1, 1))
            prior_acc[:, c * LEV:(c + 1) * LEV] = weight * (6.0 * here - around)

        result = prior_acc[...]
        for o in range(n_orbit):
            for copy in t_copies[o]:
                copy.wait_recv()
            per_group = []
            for g, d in enumerate(groups):
                total = t_send[turn, o, g]
                for k, distance in enumerate(peers):
                    theirs = (d - distance) % n_lon
                    if k > 0 and theirs in groups:
                        total = total + t_recv[turn, k - 1, o, groups.index(theirs)]
                image = jnp.zeros((SUB, rays), f32)
                for t in range(species):
                    image = image + gcol[t] * total[t:t + 1, :]
                per_group.append(image)
            result = result + back_orbit(o, per_group)
        for copy in halos[2:]:
            copy.wait_recv()
        west = result[:, :LEV] - weight * lon_halo[turn, 0]
        east = result[:, last:] - weight * lon_halo[turn, 1]
        return jnp.concatenate([west, result[:, LEV:last], east], axis=1)

    def inner(a, b):
        whole = a * b
        lanes = sum(whole[:, c * LEV:(c + 1) * LEV] for c in range(CLON))
        return jnp.sum(jnp.sum(lanes, axis=0, keepdims=True), axis=1, keepdims=True)

    def form_dots(turn):
        r = vec_r[...]
        w = ops[turn + 1] if turn + 1 < ITERS else vec_w[...]
        terms = [inner(r, r), inner(r, w)]
        if turn > 0:
            terms += [inner(r, vec_s[...]), inner(vec_d[...], w)]
        spot = lax.broadcasted_iota(jnp.int32, (1, LEV), 1)
        row = jnp.zeros((1, LEV), f32)
        for i, term in enumerate(terms):
            row = jnp.where(spot == i, term, row)
        share(turn, row)

    def share(turn, row):
        plane_sums[turn, 0] = row

        def send(k):
            pltpu.make_async_remote_copy(
                src_ref=plane_sums.at[turn, 0], dst_ref=plane_sums.at[turn, k + 1],
                send_sem=d_ssem.at[turn], recv_sem=d_rsem.at[turn],
                device_id=plane_peer(k + 1), device_id_type=MESH).start()

        each(planes - 1, send)

    def finish_dots(turn):
        others = plane_sums.at[turn, pl.ds(1, planes - 1)]
        whole = pltpu.make_async_remote_copy(
            src_ref=others, dst_ref=others, send_sem=d_ssem.at[turn], recv_sem=d_rsem.at[turn],
            device_id=plane_peer(1), device_id_type=MESH)
        whole.wait_recv()
        sent.append(whole)
        total = jnp.zeros((1, LEV), f32)
        for f in range(planes):
            total = total + plane_sums[turn, lax.rem(place + planes - f, planes)]
        return [total[:, i:i + 1] for i in range(4)]

    images = [[jnp.where(sublane < species, source[o, g], 0.0) for g in range(len(groups))]
              for o in range(n_orbit)]
    right_side = back(images)
    vec_r[...] = right_side
    ops[0] = right_side
    ops[1] = product(0)
    kept = {}

    def advance(turn):
        norm, cross, cross_s, cross_d = finish_dots(turn)
        w = ops[turn + 1] if turn + 1 < ITERS else vec_w[...]
        if turn == 0:
            kept["curvature"] = cross
            alpha = norm / cross
            direction = vec_r[...]
            moved = w
            vec_x[...] = alpha * direction
        else:
            beta = norm / kept["norm"]
            kept["beta"] = beta
            kept["curvature"] = cross + beta * (cross_s + cross_d) + beta * beta * kept["curvature"]
            alpha = norm / kept["curvature"]
            direction = vec_r[...] + beta * vec_d[...]
            moved = w + beta * vec_s[...]
            vec_x[...] = vec_x[...] + alpha * direction
        vec_r[...] = vec_r[...] - alpha * moved
        if turn < ITERS - 1:
            vec_d[...] = direction
            vec_s[...] = moved
        kept["norm"] = norm
        kept["alpha"] = alpha

    for turn in range(ITERS - 1):
        image = product(turn + 1, lambda: form_dots(turn))
        advance(turn)
        twice = image if turn == 0 else image + kept["beta"] * vec_z[...]
        vec_z[...] = twice
        moved_on = ops[turn + 1] - kept["alpha"] * twice
        if turn + 2 < ITERS:
            ops[turn + 2] = moved_on
        else:
            vec_w[...] = moved_on
    form_dots(ITERS - 1)
    advance(ITERS - 1)
    x_out[...] = vec_x[...]
    r_out[...] = vec_r[...]
    for copy in sent:
        copy.wait_send()


def body(sizes, observed, ray_start, tile_cells, tile_lengths, channel_kernel, noise_weight, prior_weight):
    n_orbit, n_lon, n_lat = sizes
    species, channels = channel_kernel.shape
    rays = ray_start.shape[0]
    rows, tile = tile_cells.shape
    groups = len(residues(NT - 1, n_lon))
    peers = len(residues(2 * (NT - 1), n_lon))
    flat = (CLAT * SUB, CLON * LEV)
    vmem = pltpu.VMEM
    dma = pltpu.SemaphoreType.DMA
    out = jax.ShapeDtypeStruct(flat, f32)
    solved, left = pl.pallas_call(
        functools.partial(kernel, sizes),
        out_shape=(out, out),
        in_specs=[pl.BlockSpec(memory_space=pltpu.HBM)] * 7,
        out_specs=[pl.BlockSpec(memory_space=pltpu.VMEM)] * 2,
        scratch_shapes=[
            vmem((channels, rays), f32),
            vmem((1, rays), jnp.int32),
            vmem((tile, rows), jnp.int32),
            vmem((tile, rows), f32),
            vmem((species, channels), f32),
            vmem((1, channels), f32),
            vmem((1, species), f32),
            dma((7,)),
            vmem((SUB, channels), f32),
            vmem((species, SUB, LEV), f32),
            vmem((SUB, LEV), f32),
            vmem((n_orbit, 2 * tile, rows), f32),
            vmem((n_orbit, CLON * LEV, groups * rays), bf16),
            vmem((n_orbit, CLON * LEV, groups * rays), bf16),
            vmem((n_orbit, SUB, groups * rays), jnp.int32),
            vmem((n_orbit, groups, SUB, rays), f32),
            vmem((ITERS,) + flat, f32),
            vmem((ITERS, 2, flat[0], LEV), f32),
            vmem((ITERS, 2, SUB, flat[1]), f32),
            vmem((ITERS, n_orbit, groups, SUB, rays), f32),
            vmem((ITERS, peers - 1, n_orbit, groups, SUB, rays), f32),
            vmem((ITERS, n_lon * n_lat, 1, LEV), f32),
        ] + [vmem(flat, f32)] * 7 + [
            dma((n_orbit, groups)), dma((n_orbit, groups)),
            dma((n_orbit,)), dma((n_orbit,)),
            dma((ITERS, 4)), dma((ITERS, 4)),
            dma((ITERS, peers, n_orbit)), dma((ITERS, peers, n_orbit)),
            dma((ITERS,)), dma((ITERS,)),
        ],
        compiler_params=pltpu.CompilerParams(
            collective_id=0, has_side_effects=True, vmem_limit_bytes=VMEM_BYTES),
    )(
        observed.T, ray_start.reshape(1, rays), tile_cells.T, tile_lengths.T,
        channel_kernel, noise_weight.reshape(1, channels), prior_weight.reshape(1, species),
    )

    def placed(field):
        shaped = field.reshape(CLAT, SUB, CLON, LEV)[:, :species]
        return shaped.transpose(1, 2, 0, 3)

    return placed(solved), placed(left)


def solution(mesh):
    sizes = tuple(mesh.shape[name] for name in ("orbit", "lon", "lat"))
    return jax.shard_map(
        functools.partial(body, sizes),
        mesh=mesh,
        in_specs=(
            P(("orbit", "lon", "lat"), None),
            P(("orbit", "lon", "lat")),
            P(("orbit", "lon", "lat"), None),
            P(("orbit", "lon", "lat"), None),
            P(),
            P(),
            P(),
        ),
        out_specs=(P(None, "lon", "lat", None), P(None, "lon", "lat", None)),
        check_vma=False,
    )
```

```python
import functools

import jax
import jax.numpy as jnp
from jax import lax
from jax.experimental import pallas as pl
from jax.experimental.pallas import tpu as pltpu
from jax.sharding import PartitionSpec as P

CLON = 4
CLAT = 8
LEV = 128
NT = 3
ITERS = 4
SUB = 8
HALF = 256
VMEM_BYTES = 60 * 1024 * 1024

highest = lax.Precision.HIGHEST
MESH = pl.DeviceIdType.MESH
f32 = jnp.float32
bf16 = jnp.bfloat16
NT_DIMS = (((1,), (1,)), ((), ()))


def each(count, step):
    if count <= 16:
        for k in range(count):
            step(k)
    else:
        lax.fori_loop(0, count, lambda k, c: (step(k), c)[1], 0)


def residues(reach, size):
    found = []
    for d in range(-reach, reach + 1):
        if d % size not in found:
            found.append(d % size)
    found.remove(0)
    return [0] + found


def kernel(sizes, observed_in, starts_in, cells_in, lengths_in, channel_in, noise_in, prior_in,
           x_out, r_out, observed, starts, cells, lengths, channel, noise, prior, load_sem,
           ck8, gcol, pw, tab, w_hi, w_lo, latkey, source, ops, lon_halo, lat_halo,
           t_send, t_recv, plane_sums, prior_acc, vec_x, vec_r, vec_w, vec_d, vec_s, vec_z,
           source_ssem, source_rsem, tab_ssem, tab_rsem, halo_ssem, halo_rsem,
           t_ssem, t_rsem, d_ssem, d_rsem):
    n_orbit, n_lon, n_lat = sizes
    reach = NT - 1
    span = 2 * NT - 1
    species, channels = channel.shape
    rays = starts.shape[1]
    tile = cells.shape[0]
    groups = residues(reach, n_lon)
    peers = residues(2 * reach, n_lon)
    group_of = [groups.index((u - reach) % n_lon) for u in range(span)]
    planes = n_lon * n_lat
    orbit = lax.axis_index("orbit")
    lon = lax.axis_index("lon")
    lat = lax.axis_index("lat")
    place = lon * n_lat + lat

    barrier = pltpu.get_barrier_semaphore()
    loads = [
        pltpu.make_async_copy(src, dst, load_sem.at[i])
        for i, (src, dst) in enumerate((
            (cells_in, cells), (lengths_in, lengths), (observed_in, observed), (channel_in, channel),
            (noise_in, noise), (starts_in, starts), (prior_in, prior)))
    ]
    for load in loads:
        load.start()

    def plane_peer(k):
        there = lax.rem(place + k, planes)
        return (orbit, lax.div(there, n_lat), lax.rem(there, n_lat))

    def greet(k):
        pl.semaphore_signal(barrier, inc=1, device_id=plane_peer(k + 1), device_id_type=MESH)

    each(planes - 1, greet)
    for o in range(1, n_orbit):
        for d in groups:
            pl.semaphore_signal(
                barrier, inc=1, device_id_type=MESH,
                device_id=(lax.rem(orbit + o, n_orbit), lax.rem(lon + d, n_lon), lat))

    for load in loads[:2]:
        load.wait()
    own_cells = cells[...]
    own_lengths = lengths[...]
    totals = jnp.zeros_like(own_lengths)
    for m in range(tile):
        totals = totals + jnp.where(own_cells == own_cells[m:m + 1, :], own_lengths[m:m + 1, :], 0.0)
    tab[orbit, 0:tile, :] = own_cells.astype(f32)
    tab[orbit, tile:2 * tile, :] = totals

    pl.semaphore_wait(barrier, planes - 1 + (n_orbit - 1) * len(groups))
    sent = []

    tab_copies = []
    for o in range(1, n_orbit):
        copy = pltpu.make_async_remote_copy(
            src_ref=tab.at[orbit], dst_ref=tab.at[orbit],
            send_sem=tab_ssem.at[o], recv_sem=tab_rsem.at[o],
            device_id=(lax.rem(orbit + o, n_orbit), lon, lat), device_id_type=MESH)
        copy.start()
        tab_copies.append(copy)
        sent.append(copy)
    for load in loads[2:]:
        load.wait()
    ck8[...] = jnp.zeros_like(ck8)
    ck8[0:species, :] = channel[...]
    kernel_rows = ck8[...]
    weighted = kernel_rows * noise[...]
    sublane = lax.broadcasted_iota(jnp.int32, (SUB, LEV), 0)
    own_source = jnp.dot(weighted, observed[...], precision=highest, preferred_element_type=f32)
    source[orbit, 0] = jnp.where(sublane == species, starts[...].astype(f32), own_source)
    source_copies = {}
    for o in range(n_orbit):
        for g, d in enumerate(groups):
            if o == 0 and g == 0:
                continue
            copy = pltpu.make_async_remote_copy(
                src_ref=source.at[orbit, 0], dst_ref=source.at[orbit, g],
                send_sem=source_ssem.at[o, g], recv_sem=source_rsem.at[o, g],
                device_id=(lax.rem(orbit + o, n_orbit), lax.rem(lon + d, n_lon), lat),
                device_id_type=MESH)
            copy.start()
            source_copies[(o, g)] = copy
            sent.append(copy)

    gram = lax.dot_general(weighted, kernel_rows, NT_DIMS, precision=highest,
                           preferred_element_type=f32)
    for t in range(species):
        gcol[t] = jnp.broadcast_to(gram[:, t:t + 1], (SUB, LEV))
    diagonal = (lax.broadcasted_iota(jnp.int32, (SUB, species), 0)
                == lax.broadcasted_iota(jnp.int32, (SUB, species), 1))
    pw_col = jnp.sum(jnp.where(diagonal, prior[...], 0.0), axis=1, keepdims=True)
    pw[...] = jnp.broadcast_to(pw_col, (SUB, LEV))

    def build(slot, g):
        first = source[slot, g, species:species + 1, :].astype(jnp.int32)
        mine = [u for u in range(span) if group_of[u] == g]
        cell = None
        for u in mine:
            own = tab[slot, 0:tile, u * rays:(u + 1) * rays]
            length = tab[slot, tile:2 * tile, u * rays:(u + 1) * rays]
            here = (first <= u) & (first + reach >= u)
            if cell is None:
                cell, total, there = own, length, here
            else:
                cell = jnp.where(here, own, cell)
                total = jnp.where(here, length, total)
                there = there | here
        cell = cell.astype(jnp.int32)
        band = lax.rem(lax.div(cell[0:1, :], LEV), CLAT)
        at = pl.ds(g * rays, rays)
        latkey[slot, :, at] = jnp.broadcast_to(jnp.where(there, band, -1), (SUB, rays))
        key = lax.div(cell, CLAT * LEV) * LEV + lax.rem(cell, LEV)
        hi = total.astype(bf16).astype(f32)
        lo = total - hi
        shape = (HALF // 16, 16, rays)
        rows = lax.broadcasted_iota(jnp.int32, shape, 0) * 16 + lax.broadcasted_iota(jnp.int32, shape, 1)
        rows = rows.astype(f32).astype(bf16)
        for half in range(CLON * LEV // HALF):
            acc_hi = jnp.zeros(shape, bf16)
            acc_lo = jnp.zeros(shape, bf16)
            near = (key - half * HALF).astype(f32)
            for m in range(tile):
                wide = lambda v: jnp.broadcast_to(v[m:m + 1, :], (16, rays)).astype(bf16)[None]
                hit = rows == wide(near)
                acc_hi = jnp.where(hit, wide(hi), acc_hi)
                acc_lo = jnp.where(hit, wide(lo), acc_lo)
            w_hi[slot, half * HALF:(half + 1) * HALF, at] = acc_hi.reshape(HALF, rays)
            w_lo[slot, half * HALF:(half + 1) * HALF, at] = acc_lo.reshape(HALF, rays)

    def await_source(o, g):
        if (o, g) != (0, 0):
            source_copies[(o, g)].wait_recv()

    for o in range(n_orbit):
        if o > 0:
            tab_copies[o - 1].wait_recv()
        for g in range(len(groups)):
            await_source(o, g)
            build(lax.rem(orbit + n_orbit - o, n_orbit), g)

    def back(images):
        total = None
        for o in range(n_orbit):
            part = back_orbit(o, images[o])
            total = part if total is None else total + part
        return total

    def back_orbit(o, per_group):
        y = jnp.concatenate(per_group, axis=1)
        y_hi = y.astype(bf16).astype(f32)
        y_lo = y - y_hi
        band = latkey[o]
        high = jnp.concatenate([jnp.where(band == b, y_hi, 0.0) for b in range(CLAT)], axis=0)
        low = jnp.concatenate([jnp.where(band == b, y_lo, 0.0) for b in range(CLAT)], axis=0)
        high = high.astype(bf16)
        both = jnp.concatenate([high, low.astype(bf16)], axis=0)
        first = lax.dot_general(both, w_hi[o], NT_DIMS, preferred_element_type=f32)
        second = lax.dot_general(high, w_lo[o], NT_DIMS, preferred_element_type=f32)
        rows = CLAT * SUB
        return first[0:rows] + (first[rows:] + second)

    def product(turn, pass_sums=None):
        v_ref = ops.at[turn]
        last = (CLON - 1) * LEV
        halos = [
            pltpu.make_async_remote_copy(
                src_ref=src, dst_ref=dst, send_sem=halo_ssem.at[turn, side],
                recv_sem=halo_rsem.at[turn, side], device_id=device, device_id_type=MESH)
            for side, (src, dst, device) in enumerate((
                (v_ref.at[(CLAT - 1) * SUB:CLAT * SUB, :], lat_halo.at[turn, 0],
                 (orbit, lon, lax.rem(lat + 1, n_lat))),
                (v_ref.at[0:SUB, :], lat_halo.at[turn, 1], (orbit, lon, lax.rem(lat + n_lat - 1, n_lat))),
                (v_ref.at[:, last:last + LEV], lon_halo.at[turn, 0],
                 (orbit, lax.rem(lon + 1, n_lon), lat)),
                (v_ref.at[:, 0:LEV], lon_halo.at[turn, 1],
                 (orbit, lax.rem(lon + n_lon - 1, n_lon), lat)),
            ))
        ]
        sent.extend(halos)
        for copy in halos[:2]:
            copy.start()
        v = v_ref[...]
        rows = CLAT * SUB
        v_high = v.astype(bf16)
        t_copies = [[] for _ in range(n_orbit)]
        v_both = jnp.concatenate([v_high, (v - v_high.astype(f32)).astype(bf16)], axis=0)
        for o in range(n_orbit):
            first = jnp.dot(v_both, w_hi[o], preferred_element_type=f32)
            second = jnp.dot(v_high, w_lo[o], preferred_element_type=f32)
            sums = first[0:rows] + (first[rows:] + second)
            band = latkey[o]
            picked = jnp.zeros((SUB, len(groups) * rays), f32)
            for b in range(CLAT):
                picked = jnp.where(band == b, sums[b * SUB:(b + 1) * SUB], picked)
            for g in range(len(groups)):
                t_send[turn, o, g] = picked[:, g * rays:(g + 1) * rays]
            for k, distance in enumerate(peers):
                if k == 0:
                    continue
                copy = pltpu.make_async_remote_copy(
                    src_ref=t_send.at[turn, o], dst_ref=t_recv.at[turn, k - 1, o],
                    send_sem=t_ssem.at[turn, k, o], recv_sem=t_rsem.at[turn, k, o],
                    device_id=(orbit, lax.rem(lon + distance, n_lon), lat), device_id_type=MESH)
                copy.start()
                t_copies[o].append(copy)
                sent.append(copy)

        for copy in halos[2:]:
            copy.start()
        if pass_sums is not None:
            pass_sums()
        for copy in halos[:2]:
            copy.wait_recv()
        lane = lax.broadcasted_iota(jnp.int32, (rows, LEV), 1)
        weight = jnp.concatenate([pw[...]] * CLAT, axis=0)
        column = lambda c: v_ref[:, c * LEV:(c + 1) * LEV]
        for c in range(CLON):
            here = column(c)
            south = jnp.where(lat == 0, 0.0, lat_halo[turn, 0, :, c * LEV:(c + 1) * LEV])
            north = jnp.where(lat == n_lat - 1, 0.0, lat_halo[turn, 1, :, c * LEV:(c + 1) * LEV])
            around = jnp.concatenate([south, here[:-SUB]], axis=0)
            around = around + jnp.concatenate([here[SUB:], north], axis=0)
            for beside in (c - 1, c + 1):
                if 0 <= beside < CLON:
                    around = around + column(beside)
            around = around + jnp.where(lane == 0, 0.0, pltpu.roll(here, 1, 1))
            around = around + jnp.where(lane == LEV - 1, 0.0, pltpu.roll(here, LEV - 1, 1))
            prior_acc[:, c * LEV:(c + 1) * LEV] = weight * (6.0 * here - around)

        result = prior_acc[...]
        for o in range(n_orbit):
            for copy in t_copies[o]:
                copy.wait_recv()
            per_group = []
            for g, d in enumerate(groups):
                total = t_send[turn, o, g]
                for k, distance in enumerate(peers):
                    theirs = (d - distance) % n_lon
                    if k > 0 and theirs in groups:
                        total = total + t_recv[turn, k - 1, o, groups.index(theirs)]
                image = jnp.zeros((SUB, rays), f32)
                for t in range(species):
                    image = image + gcol[t] * total[t:t + 1, :]
                per_group.append(image)
            result = result + back_orbit(o, per_group)
        for copy in halos[2:]:
            copy.wait_recv()
        west = result[:, :LEV] - weight * lon_halo[turn, 0]
        east = result[:, last:] - weight * lon_halo[turn, 1]
        return jnp.concatenate([west, result[:, LEV:last], east], axis=1)

    def inner(a, b):
        whole = a * b
        lanes = sum(whole[:, c * LEV:(c + 1) * LEV] for c in range(CLON))
        return jnp.sum(jnp.sum(lanes, axis=0, keepdims=True), axis=1, keepdims=True)

    def form_dots(turn):
        r = vec_r[...]
        w = ops[turn + 1] if turn + 1 < ITERS else vec_w[...]
        terms = [inner(r, r), inner(r, w)]
        if turn > 0:
            terms += [inner(r, vec_s[...]), inner(vec_d[...], w)]
        spot = lax.broadcasted_iota(jnp.int32, (1, LEV), 1)
        row = jnp.zeros((1, LEV), f32)
        for i, term in enumerate(terms):
            row = jnp.where(spot == i, term, row)
        plane_sums[turn, 0] = row

    def share(turn):
        def send(k):
            pltpu.make_async_remote_copy(
                src_ref=plane_sums.at[turn, 0], dst_ref=plane_sums.at[turn, k + 1],
                send_sem=d_ssem.at[turn], recv_sem=d_rsem.at[turn],
                device_id=plane_peer(k + 1), device_id_type=MESH).start()

        each(planes - 1, send)

    def finish_dots(turn):
        others = plane_sums.at[turn, pl.ds(1, planes - 1)]
        whole = pltpu.make_async_remote_copy(
            src_ref=others, dst_ref=others, send_sem=d_ssem.at[turn], recv_sem=d_rsem.at[turn],
            device_id=plane_peer(1), device_id_type=MESH)
        whole.wait_recv()
        sent.append(whole)
        total = jnp.zeros((1, LEV), f32)
        for f in range(planes):
            total = total + plane_sums[turn, lax.rem(place + planes - f, planes)]
        return [total[:, i:i + 1] for i in range(4)]

    images = [[jnp.where(sublane < species, source[o, g], 0.0) for g in range(len(groups))]
              for o in range(n_orbit)]
    right_side = back(images)
    vec_r[...] = right_side
    ops[0] = right_side
    ops[1] = product(0)
    kept = {}

    def advance(turn):
        norm, cross, cross_s, cross_d = finish_dots(turn)
        w = ops[turn + 1] if turn + 1 < ITERS else vec_w[...]
        if turn == 0:
            kept["curvature"] = cross
            alpha = norm / cross
            direction = vec_r[...]
            moved = w
        else:
            beta = norm / kept["norm"]
            kept["beta"] = beta
            kept["curvature"] = cross + beta * (cross_s + cross_d) + beta * beta * kept["curvature"]
            alpha = norm / kept["curvature"]
            direction = vec_r[...] + beta * vec_d[...]
            moved = w + beta * vec_s[...]
        vec_r[...] = vec_r[...] - alpha * moved
        if turn < ITERS - 1:
            vec_d[...] = direction
            vec_s[...] = moved
        kept["norm"] = norm
        kept["alpha"] = alpha
        if turn == ITERS - 1:
            vec_x[...] = vec_x[...] + alpha * direction

    def move_solution(turn):
        if turn == 0:
            vec_x[...] = kept["alpha"] * vec_d[...]
        elif turn > 0:
            vec_x[...] = vec_x[...] + kept["alpha"] * vec_d[...]

    for turn in range(ITERS - 1):
        form_dots(turn)
        image = product(turn + 1, lambda: (share(turn), move_solution(turn - 1)))
        advance(turn)
        twice = image if turn == 0 else image + kept["beta"] * vec_z[...]
        vec_z[...] = twice
        moved_on = ops[turn + 1] - kept["alpha"] * twice
        if turn + 2 < ITERS:
            ops[turn + 2] = moved_on
        else:
            vec_w[...] = moved_on
    form_dots(ITERS - 1)
    share(ITERS - 1)
    move_solution(ITERS - 2)
    advance(ITERS - 1)
    x_out[...] = vec_x[...]
    r_out[...] = vec_r[...]
    for copy in sent:
        copy.wait_send()


def body(sizes, observed, ray_start, tile_cells, tile_lengths, channel_kernel, noise_weight, prior_weight):
    n_orbit, n_lon, n_lat = sizes
    species, channels = channel_kernel.shape
    rays = ray_start.shape[0]
    rows, tile = tile_cells.shape
    groups = len(residues(NT - 1, n_lon))
    peers = len(residues(2 * (NT - 1), n_lon))
    flat = (CLAT * SUB, CLON * LEV)
    vmem = pltpu.VMEM
    dma = pltpu.SemaphoreType.DMA
    out = jax.ShapeDtypeStruct(flat, f32)
    solved, left = pl.pallas_call(
        functools.partial(kernel, sizes),
        out_shape=(out, out),
        in_specs=[pl.BlockSpec(memory_space=pltpu.HBM)] * 7,
        out_specs=[pl.BlockSpec(memory_space=pltpu.VMEM)] * 2,
        scratch_shapes=[
            vmem((channels, rays), f32),
            vmem((1, rays), jnp.int32),
            vmem((tile, rows), jnp.int32),
            vmem((tile, rows), f32),
            vmem((species, channels), f32),
            vmem((1, channels), f32),
            vmem((1, species), f32),
            dma((7,)),
            vmem((SUB, channels), f32),
            vmem((species, SUB, LEV), f32),
            vmem((SUB, LEV), f32),
            vmem((n_orbit, 2 * tile, rows), f32),
            vmem((n_orbit, CLON * LEV, groups * rays), bf16),
            vmem((n_orbit, CLON * LEV, groups * rays), bf16),
            vmem((n_orbit, SUB, groups * rays), jnp.int32),
            vmem((n_orbit, groups, SUB, rays), f32),
            vmem((ITERS,) + flat, f32),
            vmem((ITERS, 2, flat[0], LEV), f32),
            vmem((ITERS, 2, SUB, flat[1]), f32),
            vmem((ITERS, n_orbit, groups, SUB, rays), f32),
            vmem((ITERS, peers - 1, n_orbit, groups, SUB, rays), f32),
            vmem((ITERS, n_lon * n_lat, 1, LEV), f32),
        ] + [vmem(flat, f32)] * 7 + [
            dma((n_orbit, groups)), dma((n_orbit, groups)),
            dma((n_orbit,)), dma((n_orbit,)),
            dma((ITERS, 4)), dma((ITERS, 4)),
            dma((ITERS, peers, n_orbit)), dma((ITERS, peers, n_orbit)),
            dma((ITERS,)), dma((ITERS,)),
        ],
        compiler_params=pltpu.CompilerParams(
            collective_id=0, has_side_effects=True, vmem_limit_bytes=VMEM_BYTES),
    )(
        observed.T, ray_start.reshape(1, rays), tile_cells.T, tile_lengths.T,
        channel_kernel, noise_weight.reshape(1, channels), prior_weight.reshape(1, species),
    )

    def placed(field):
        shaped = field.reshape(CLAT, SUB, CLON, LEV)[:, :species]
        return shaped.transpose(1, 2, 0, 3)

    return placed(solved), placed(left)


def solution(mesh):
    sizes = tuple(mesh.shape[name] for name in ("orbit", "lon", "lat"))
    return jax.shard_map(
        functools.partial(body, sizes),
        mesh=mesh,
        in_specs=(
            P(("orbit", "lon", "lat"), None),
            P(("orbit", "lon", "lat")),
            P(("orbit", "lon", "lat"), None),
            P(("orbit", "lon", "lat"), None),
            P(),
            P(),
            P(),
        ),
        out_specs=(P(None, "lon", "lat", None), P(None, "lon", "lat", None)),
        check_vma=False,
    )
```

```python
import functools

import jax
import jax.numpy as jnp
from jax import lax
from jax.experimental import pallas as pl
from jax.experimental.pallas import tpu as pltpu
from jax.sharding import PartitionSpec as P

CLON = 4
CLAT = 8
LEV = 128
NT = 3
ITERS = 4
SUB = 8
HALF = 256
VMEM_BYTES = 60 * 1024 * 1024

highest = lax.Precision.HIGHEST
MESH = pl.DeviceIdType.MESH
f32 = jnp.float32
bf16 = jnp.bfloat16
NT_DIMS = (((1,), (1,)), ((), ()))


def each(count, step):
    if count <= 16:
        for k in range(count):
            step(k)
    else:
        lax.fori_loop(0, count, lambda k, c: (step(k), c)[1], 0)


def residues(reach, size):
    found = []
    for d in range(-reach, reach + 1):
        if d % size not in found:
            found.append(d % size)
    found.remove(0)
    return [0] + found


def kernel(sizes, observed_in, starts_in, cells_in, lengths_in, channel_in, noise_in, prior_in,
           x_out, r_out, observed, starts, cells, lengths, channel, noise, prior, load_sem,
           ck8, gcol, pw, tab, w_hi, w_lo, latkey, source, ops, lon_halo, lat_halo,
           t_send, t_recv, plane_sums, prior_acc, vec_x, vec_r, vec_w, vec_d, vec_s, vec_z,
           source_ssem, source_rsem, tab_ssem, tab_rsem, halo_ssem, halo_rsem,
           t_ssem, t_rsem, d_ssem, d_rsem):
    n_orbit, n_lon, n_lat = sizes
    reach = NT - 1
    span = 2 * NT - 1
    species, channels = channel.shape
    rays = starts.shape[1]
    tile = cells.shape[0]
    groups = residues(reach, n_lon)
    peers = residues(2 * reach, n_lon)
    group_of = [groups.index((u - reach) % n_lon) for u in range(span)]
    planes = n_lon * n_lat
    orbit = lax.axis_index("orbit")
    lon = lax.axis_index("lon")
    lat = lax.axis_index("lat")
    place = lon * n_lat + lat

    barrier = pltpu.get_barrier_semaphore()
    loads = [
        pltpu.make_async_copy(src, dst, load_sem.at[i])
        for i, (src, dst) in enumerate((
            (cells_in, cells), (lengths_in, lengths), (observed_in, observed), (channel_in, channel),
            (noise_in, noise), (starts_in, starts), (prior_in, prior)))
    ]
    for load in loads:
        load.start()

    def plane_peer(k):
        there = lax.rem(place + k, planes)
        return (orbit, lax.div(there, n_lat), lax.rem(there, n_lat))

    def greet(k):
        pl.semaphore_signal(barrier, inc=1, device_id=plane_peer(k + 1), device_id_type=MESH)

    each(planes - 1, greet)
    for o in range(1, n_orbit):
        for d in groups:
            pl.semaphore_signal(
                barrier, inc=1, device_id_type=MESH,
                device_id=(lax.rem(orbit + o, n_orbit), lax.rem(lon + d, n_lon), lat))

    for load in loads[:2]:
        load.wait()
    own_cells = cells[...]
    own_lengths = lengths[...]
    totals = jnp.zeros_like(own_lengths)
    for m in range(tile):
        totals = totals + jnp.where(own_cells == own_cells[m:m + 1, :], own_lengths[m:m + 1, :], 0.0)
    tab[orbit, 0:tile, :] = own_cells.astype(f32)
    tab[orbit, tile:2 * tile, :] = totals

    pl.semaphore_wait(barrier, planes - 1 + (n_orbit - 1) * len(groups))
    sent = []

    tab_copies = []
    for o in range(1, n_orbit):
        copy = pltpu.make_async_remote_copy(
            src_ref=tab.at[orbit], dst_ref=tab.at[orbit],
            send_sem=tab_ssem.at[o], recv_sem=tab_rsem.at[o],
            device_id=(lax.rem(orbit + o, n_orbit), lon, lat), device_id_type=MESH)
        copy.start()
        tab_copies.append(copy)
        sent.append(copy)
    for load in loads[2:]:
        load.wait()
    ck8[...] = jnp.zeros_like(ck8)
    ck8[0:species, :] = channel[...]
    kernel_rows = ck8[...]
    weighted = kernel_rows * noise[...]
    sublane = lax.broadcasted_iota(jnp.int32, (SUB, LEV), 0)
    own_source = jnp.dot(weighted, observed[...], precision=highest, preferred_element_type=f32)
    source[orbit, 0] = jnp.where(sublane == species, starts[...].astype(f32), own_source)
    source_copies = {}
    for o in range(n_orbit):
        for g, d in enumerate(groups):
            if o == 0 and g == 0:
                continue
            copy = pltpu.make_async_remote_copy(
                src_ref=source.at[orbit, 0], dst_ref=source.at[orbit, g],
                send_sem=source_ssem.at[o, g], recv_sem=source_rsem.at[o, g],
                device_id=(lax.rem(orbit + o, n_orbit), lax.rem(lon + d, n_lon), lat),
                device_id_type=MESH)
            copy.start()
            source_copies[(o, g)] = copy
            sent.append(copy)

    gram = lax.dot_general(weighted, kernel_rows, NT_DIMS, precision=highest,
                           preferred_element_type=f32)
    for t in range(species):
        gcol[t] = jnp.broadcast_to(gram[:, t:t + 1], (SUB, LEV))
    diagonal = (lax.broadcasted_iota(jnp.int32, (SUB, species), 0)
                == lax.broadcasted_iota(jnp.int32, (SUB, species), 1))
    pw_col = jnp.sum(jnp.where(diagonal, prior[...], 0.0), axis=1, keepdims=True)
    pw[...] = jnp.broadcast_to(pw_col, (SUB, LEV))

    def build(slot, g):
        first = source[slot, g, species:species + 1, :].astype(jnp.int32)
        mine = [u for u in range(span) if group_of[u] == g]
        cell = None
        for u in mine:
            own = tab[slot, 0:tile, u * rays:(u + 1) * rays]
            length = tab[slot, tile:2 * tile, u * rays:(u + 1) * rays]
            here = (first <= u) & (first + reach >= u)
            if cell is None:
                cell, total, there = own, length, here
            else:
                cell = jnp.where(here, own, cell)
                total = jnp.where(here, length, total)
                there = there | here
        cell = cell.astype(jnp.int32)
        band = lax.rem(lax.div(cell[0:1, :], LEV), CLAT)
        at = pl.ds(g * rays, rays)
        latkey[slot, :, at] = jnp.broadcast_to(jnp.where(there, band, -1), (SUB, rays))
        key = lax.div(cell, CLAT * LEV) * LEV + lax.rem(cell, LEV)
        hi = total.astype(bf16).astype(f32)
        lo = total - hi
        shape = (HALF // 16, 16, rays)
        rows = lax.broadcasted_iota(jnp.int32, shape, 0) * 16 + lax.broadcasted_iota(jnp.int32, shape, 1)
        rows = rows.astype(f32).astype(bf16)
        for half in range(CLON * LEV // HALF):
            acc_hi = jnp.zeros(shape, bf16)
            acc_lo = jnp.zeros(shape, bf16)
            near = (key - half * HALF).astype(f32)
            for m in range(tile):
                wide = lambda v: jnp.broadcast_to(v[m:m + 1, :], (16, rays)).astype(bf16)[None]
                hit = rows == wide(near)
                acc_hi = jnp.where(hit, wide(hi), acc_hi)
                acc_lo = jnp.where(hit, wide(lo), acc_lo)
            w_hi[slot, half * HALF:(half + 1) * HALF, at] = acc_hi.reshape(HALF, rays)
            w_lo[slot, half * HALF:(half + 1) * HALF, at] = acc_lo.reshape(HALF, rays)

    def await_source(o, g):
        if (o, g) != (0, 0):
            source_copies[(o, g)].wait_recv()

    for o in range(n_orbit):
        if o > 0:
            tab_copies[o - 1].wait_recv()
        for g in range(len(groups)):
            await_source(o, g)
            build(lax.rem(orbit + n_orbit - o, n_orbit), g)

    def back(images):
        total = None
        for o in range(n_orbit):
            part = back_orbit(o, images[o])
            total = part if total is None else total + part
        return total

    def back_orbit(o, per_group):
        y = jnp.concatenate(per_group, axis=1)
        y_hi = y.astype(bf16).astype(f32)
        y_lo = y - y_hi
        band = latkey[o]
        high = jnp.concatenate([jnp.where(band == b, y_hi, 0.0) for b in range(CLAT)], axis=0)
        low = jnp.concatenate([jnp.where(band == b, y_lo, 0.0) for b in range(CLAT)], axis=0)
        high = high.astype(bf16)
        both = jnp.concatenate([high, low.astype(bf16)], axis=0)
        first = lax.dot_general(both, w_hi[o], NT_DIMS, preferred_element_type=f32)
        second = lax.dot_general(high, w_lo[o], NT_DIMS, preferred_element_type=f32)
        rows = CLAT * SUB
        return first[0:rows] + (first[rows:] + second)

    def product(turn, pass_sums=None):
        v_ref = ops.at[turn]
        last = (CLON - 1) * LEV
        halos = [
            pltpu.make_async_remote_copy(
                src_ref=src, dst_ref=dst, send_sem=halo_ssem.at[turn, side],
                recv_sem=halo_rsem.at[turn, side], device_id=device, device_id_type=MESH)
            for side, (src, dst, device) in enumerate((
                (v_ref.at[(CLAT - 1) * SUB:CLAT * SUB, :], lat_halo.at[turn, 0],
                 (orbit, lon, lax.rem(lat + 1, n_lat))),
                (v_ref.at[0:SUB, :], lat_halo.at[turn, 1], (orbit, lon, lax.rem(lat + n_lat - 1, n_lat))),
                (v_ref.at[:, last:last + LEV], lon_halo.at[turn, 0],
                 (orbit, lax.rem(lon + 1, n_lon), lat)),
                (v_ref.at[:, 0:LEV], lon_halo.at[turn, 1],
                 (orbit, lax.rem(lon + n_lon - 1, n_lon), lat)),
            ))
        ]
        sent.extend(halos)
        for copy in halos[:2]:
            copy.start()
        v = v_ref[...]
        rows = CLAT * SUB
        v_high = v.astype(bf16)
        t_copies = [[] for _ in range(n_orbit)]
        v_both = jnp.concatenate([v_high, (v - v_high.astype(f32)).astype(bf16)], axis=0)
        for o in range(n_orbit):
            first = jnp.dot(v_both, w_hi[o], preferred_element_type=f32)
            second = jnp.dot(v_high, w_lo[o], preferred_element_type=f32)
            sums = first[0:rows] + (first[rows:] + second)
            band = latkey[o]
            picked = jnp.zeros((SUB, len(groups) * rays), f32)
            for b in range(CLAT):
                picked = jnp.where(band == b, sums[b * SUB:(b + 1) * SUB], picked)
            for g in range(len(groups)):
                t_send[turn, o, g] = picked[:, g * rays:(g + 1) * rays]
            for k, distance in enumerate(peers):
                if k == 0:
                    continue
                copy = pltpu.make_async_remote_copy(
                    src_ref=t_send.at[turn, o], dst_ref=t_recv.at[turn, k - 1, o],
                    send_sem=t_ssem.at[turn, k, o], recv_sem=t_rsem.at[turn, k, o],
                    device_id=(orbit, lax.rem(lon + distance, n_lon), lat), device_id_type=MESH)
                copy.start()
                t_copies[o].append(copy)
                sent.append(copy)

        for copy in halos[2:]:
            copy.start()
        if pass_sums is not None:
            pass_sums()
        for copy in halos[:2]:
            copy.wait_recv()
        lane = lax.broadcasted_iota(jnp.int32, (rows, LEV), 1)
        weight = jnp.concatenate([pw[...]] * CLAT, axis=0)
        column = lambda c: v_ref[:, c * LEV:(c + 1) * LEV]
        for c in range(CLON):
            here = column(c)
            south = jnp.where(lat == 0, 0.0, lat_halo[turn, 0, :, c * LEV:(c + 1) * LEV])
            north = jnp.where(lat == n_lat - 1, 0.0, lat_halo[turn, 1, :, c * LEV:(c + 1) * LEV])
            around = jnp.concatenate([south, here[:-SUB]], axis=0)
            around = around + jnp.concatenate([here[SUB:], north], axis=0)
            for beside in (c - 1, c + 1):
                if 0 <= beside < CLON:
                    around = around + column(beside)
            around = around + jnp.where(lane == 0, 0.0, pltpu.roll(here, 1, 1))
            around = around + jnp.where(lane == LEV - 1, 0.0, pltpu.roll(here, LEV - 1, 1))
            prior_acc[:, c * LEV:(c + 1) * LEV] = weight * (6.0 * here - around)

        result = prior_acc[...]
        for o in range(n_orbit):
            for copy in t_copies[o]:
                copy.wait_recv()
            per_group = []
            for g, d in enumerate(groups):
                total = t_send[turn, o, g]
                for k, distance in enumerate(peers):
                    theirs = (d - distance) % n_lon
                    if k > 0 and theirs in groups:
                        total = total + t_recv[turn, k - 1, o, groups.index(theirs)]
                image = jnp.zeros((SUB, rays), f32)
                for t in range(species):
                    image = image + gcol[t] * total[t:t + 1, :]
                per_group.append(image)
            result = result + back_orbit(o, per_group)
        for copy in halos[2:]:
            copy.wait_recv()
        west = result[:, :LEV] - weight * lon_halo[turn, 0]
        east = result[:, last:] - weight * lon_halo[turn, 1]
        return jnp.concatenate([west, result[:, LEV:last], east], axis=1)

    def inner(a, b):
        whole = a * b
        lanes = sum(whole[:, c * LEV:(c + 1) * LEV] for c in range(CLON))
        return jnp.sum(jnp.sum(lanes, axis=0, keepdims=True), axis=1, keepdims=True)

    def form_dots(turn):
        r = vec_r[...]
        w = ops[turn + 1] if turn + 1 < ITERS else vec_w[...]
        terms = [inner(r, r), inner(r, w)]
        if turn > 0:
            terms += [inner(r, vec_s[...]), inner(vec_d[...], w)]
        spot = lax.broadcasted_iota(jnp.int32, (1, LEV), 1)
        row = jnp.zeros((1, LEV), f32)
        for i, term in enumerate(terms):
            row = jnp.where(spot == i, term, row)
        plane_sums[turn, 0] = row

    def share(turn):
        def send(k):
            pltpu.make_async_remote_copy(
                src_ref=plane_sums.at[turn, 0], dst_ref=plane_sums.at[turn, k + 1],
                send_sem=d_ssem.at[turn], recv_sem=d_rsem.at[turn],
                device_id=plane_peer(k + 1), device_id_type=MESH).start()

        each(planes - 1, send)

    def finish_dots(turn):
        others = plane_sums.at[turn, pl.ds(1, planes - 1)]
        whole = pltpu.make_async_remote_copy(
            src_ref=others, dst_ref=others, send_sem=d_ssem.at[turn], recv_sem=d_rsem.at[turn],
            device_id=plane_peer(1), device_id_type=MESH)
        whole.wait_recv()
        sent.append(whole)
        total = jnp.zeros((1, LEV), f32)
        for f in range(planes):
            total = total + plane_sums[turn, lax.rem(place + planes - f, planes)]
        return [total[:, i:i + 1] for i in range(4)]

    images = [[jnp.where(sublane < species, source[o, g], 0.0) for g in range(len(groups))]
              for o in range(n_orbit)]
    right_side = back(images)
    vec_r[...] = right_side
    ops[0] = right_side
    ops[1] = product(0)
    kept = {}

    def advance(turn):
        norm, cross, cross_s, cross_d = finish_dots(turn)
        w = ops[turn + 1] if turn + 1 < ITERS else vec_w[...]
        if turn == 0:
            kept["curvature"] = cross
            alpha = norm / cross
            direction = vec_r[...]
            moved = w
        else:
            beta = norm / kept["norm"]
            kept["beta"] = beta
            kept["curvature"] = cross + beta * (cross_s + cross_d) + beta * beta * kept["curvature"]
            alpha = norm / kept["curvature"]
            direction = vec_r[...] + beta * vec_d[...]
            moved = w + beta * vec_s[...]
        vec_r[...] = vec_r[...] - alpha * moved
        if turn < ITERS - 1:
            vec_d[...] = direction
            vec_s[...] = moved
        kept["norm"] = norm
        kept["alpha"] = alpha
        if turn == ITERS - 1:
            vec_x[...] = vec_x[...] + alpha * direction

    def move_solution(turn):
        if turn == 0:
            vec_x[...] = kept["alpha"] * vec_d[...]
        elif turn > 0:
            vec_x[...] = vec_x[...] + kept["alpha"] * vec_d[...]

    for turn in range(ITERS - 1):
        form_dots(turn)
        share(turn)
        image = product(turn + 1, lambda: move_solution(turn - 1))
        advance(turn)
        twice = image if turn == 0 else image + kept["beta"] * vec_z[...]
        vec_z[...] = twice
        moved_on = ops[turn + 1] - kept["alpha"] * twice
        if turn + 2 < ITERS:
            ops[turn + 2] = moved_on
        else:
            vec_w[...] = moved_on
    form_dots(ITERS - 1)
    share(ITERS - 1)
    move_solution(ITERS - 2)
    advance(ITERS - 1)
    x_out[...] = vec_x[...]
    r_out[...] = vec_r[...]
    for copy in sent:
        copy.wait_send()


def body(sizes, observed, ray_start, tile_cells, tile_lengths, channel_kernel, noise_weight, prior_weight):
    n_orbit, n_lon, n_lat = sizes
    species, channels = channel_kernel.shape
    rays = ray_start.shape[0]
    rows, tile = tile_cells.shape
    groups = len(residues(NT - 1, n_lon))
    peers = len(residues(2 * (NT - 1), n_lon))
    flat = (CLAT * SUB, CLON * LEV)
    vmem = pltpu.VMEM
    dma = pltpu.SemaphoreType.DMA
    out = jax.ShapeDtypeStruct(flat, f32)
    solved, left = pl.pallas_call(
        functools.partial(kernel, sizes),
        out_shape=(out, out),
        in_specs=[pl.BlockSpec(memory_space=pltpu.HBM)] * 7,
        out_specs=[pl.BlockSpec(memory_space=pltpu.VMEM)] * 2,
        scratch_shapes=[
            vmem((channels, rays), f32),
            vmem((1, rays), jnp.int32),
            vmem((tile, rows), jnp.int32),
            vmem((tile, rows), f32),
            vmem((species, channels), f32),
            vmem((1, channels), f32),
            vmem((1, species), f32),
            dma((7,)),
            vmem((SUB, channels), f32),
            vmem((species, SUB, LEV), f32),
            vmem((SUB, LEV), f32),
            vmem((n_orbit, 2 * tile, rows), f32),
            vmem((n_orbit, CLON * LEV, groups * rays), bf16),
            vmem((n_orbit, CLON * LEV, groups * rays), bf16),
            vmem((n_orbit, SUB, groups * rays), jnp.int32),
            vmem((n_orbit, groups, SUB, rays), f32),
            vmem((ITERS,) + flat, f32),
            vmem((ITERS, 2, flat[0], LEV), f32),
            vmem((ITERS, 2, SUB, flat[1]), f32),
            vmem((ITERS, n_orbit, groups, SUB, rays), f32),
            vmem((ITERS, peers - 1, n_orbit, groups, SUB, rays), f32),
            vmem((ITERS, n_lon * n_lat, 1, LEV), f32),
        ] + [vmem(flat, f32)] * 7 + [
            dma((n_orbit, groups)), dma((n_orbit, groups)),
            dma((n_orbit,)), dma((n_orbit,)),
            dma((ITERS, 4)), dma((ITERS, 4)),
            dma((ITERS, peers, n_orbit)), dma((ITERS, peers, n_orbit)),
            dma((ITERS,)), dma((ITERS,)),
        ],
        compiler_params=pltpu.CompilerParams(
            collective_id=0, has_side_effects=True, vmem_limit_bytes=VMEM_BYTES),
    )(
        observed.T, ray_start.reshape(1, rays), tile_cells.T, tile_lengths.T,
        channel_kernel, noise_weight.reshape(1, channels), prior_weight.reshape(1, species),
    )

    def placed(field):
        shaped = field.reshape(CLAT, SUB, CLON, LEV)[:, :species]
        return shaped.transpose(1, 2, 0, 3)

    return placed(solved), placed(left)


def solution(mesh):
    sizes = tuple(mesh.shape[name] for name in ("orbit", "lon", "lat"))
    return jax.shard_map(
        functools.partial(body, sizes),
        mesh=mesh,
        in_specs=(
            P(("orbit", "lon", "lat"), None),
            P(("orbit", "lon", "lat")),
            P(("orbit", "lon", "lat"), None),
            P(("orbit", "lon", "lat"), None),
            P(),
            P(),
            P(),
        ),
        out_specs=(P(None, "lon", "lat", None), P(None, "lon", "lat", None)),
        check_vma=False,
    )
```
